256 devices in a mesh: group: 16 (over z, core), head: 16 (over y, x).
Axes of the slice: x: 4, y: 4, z: 8, core: 2. Of those that a mesh axis runs over, the one named last changes fastest.
Arguments:
- hidden_in: bfloat16 [2, 1024, 7168], P(None, ('group', 'head')), may hold values from -6 to 6
- queries: bfloat16 [2, 1024, 64, 576], P(None, ('group', 'head')), may hold values from -6 to 6
- fresh: bfloat16 [2, 1024, 576], P(None, ('group', 'head')), may hold values from -6 to 6
- res_cache: bfloat16 [512, 1024, 576], P(('group', 'head')), may hold values from -8 to 8
- res_len: int32 [512], P(('group', 'head')), may hold values from 1 to 1024, as said below
- pre_cache: bfloat16 [16, 32, 128, 576], P('head', None, 'group'), may hold values from -8 to 8
- pre_len: int32 [16, 32], P('head'), may hold values from 1 to 128, as said below
- arrival: int32 [16, 32], P('head'), may hold values from 0 to 31, each once within a row
- w_uv: bfloat16 [64, 512, 128], P('head'), may hold values from -0.25 to 0.25
- w_o: bfloat16 [8192, 7168], P('head', 'group'), may hold values from -0.0625 to 0.0625
- norm_gain: float32 [7168], replicated, may hold values from 0.5 to 1.5
- expert_ids: int32 [2, 1024, 8], P(None, 'group'), may hold values from 0 to 255, all different within a row; in each aligned block of 64 rows (0 to 63, 64 to 127, ..., all dimensions but the last counted through in order) at most 4 rows name the same one
- route_weight: float32 [2, 1024, 8], P(None, 'group'), may hold values from 0.2 to 1
- w_gu: bfloat16 [16, 2, 7168, 2048], P('head', None, None, 'group'), may hold values from -0.0625 to 0.0625
- w_down: bfloat16 [16, 2048, 7168], P('head', None, 'group'), may hold values from -0.125 to 0.125
Outputs:
- layer_out: bfloat16 [2, 1024, 7168], P(None, ('group', 'head'))
The draws below stay inside these ranges and needn't reach their ends.
Inputs may be any that keep to these rules, and one draw needn't show every extreme that they name: `res_len`: some resident row has length exactly 1024. `pre_len`: some new request has length exactly 128. Each row of arrival is a permutation of 0 to 31. `expert_ids`: each row names 8 different experts. Within the rows of one group in one step (aligned blocks of 64 rows) no expert is named by more than 4 rows.
All inputs are finite; a program needn't handle non-finite values.
Results may differ from the reference program's by a relative error of at most 0.0065.
Values may be sent and summed in bfloat16 or wider, within the bound.
No kernel may reach another device: no remote copies, remote signals or barrier semaphores. Data moves between devices by JAX's collectives and lax.ppermute only.
A program may use at most 64 MiB of HBM per device.

```python
import math
import jax
import jax.numpy as jnp
import numpy as np
from jax import lax

D = 7168
HEADS = 64
LAT = 512
ROPE = 64
KD = 576
VD = 128
FFE = 2048
EXPERTS = 256
TOPK = 8
EXP_WIN = 16
CAP = 4
STEPS = 2
R_DEV = 2
NEW_DEV = 2
ROWS_DEV = 4
CTX = 1024
PRE = 128
NEW_COL = 32
ROWS = 1024
ROWS_RES = 512
N_GROUP = 16
N_HEAD = 16


def draw_queries(key, part):
    key = jax.random.fold_in(key, 47)
    key_base = jax.random.fold_in(key, 0)
    base = jnp.clip(0.5 * jax.random.normal(key_base, (STEPS, ROWS, HEADS, KD), jnp.float32), -4.0, 4.0)
    result = base
    return result.astype(jnp.bfloat16)


def draw_res_cache(key, part):
    key = jax.random.fold_in(key, 31)
    key_base = jax.random.fold_in(key, 0)
    base = jnp.clip(jax.random.normal(key_base, (ROWS_RES, CTX, KD), jnp.float32), -6.0, 6.0)
    result = base
    return result.astype(jnp.bfloat16)


def draw_pre_cache(key, part):
    key = jax.random.fold_in(key, 37)
    key_base = jax.random.fold_in(key, 0)
    base = jnp.clip(jax.random.normal(key_base, (N_HEAD, NEW_COL, PRE, KD), jnp.float32), -6.0, 6.0)
    result = base
    return result.astype(jnp.bfloat16)


def draw_res_len(key, part):
    key = jax.random.fold_in(key, 11)
    key_values, key_place = jax.random.split(key)
    values = jax.random.randint(key_values, (ROWS_RES,), 1, CTX + 1)
    chosen_row = jax.random.randint(key_place, (), 0, ROWS_RES)
    return jnp.where(jnp.arange(ROWS_RES) == chosen_row, CTX, values).astype(jnp.int32)


def draw_pre_len(key, part):
    key = jax.random.fold_in(key, 23)
    key_values, key_place = jax.random.split(key)
    values = jax.random.randint(key_values, (N_HEAD * NEW_COL,), 1, PRE + 1)
    chosen_row = jax.random.randint(key_place, (), 0, N_HEAD * NEW_COL)
    values = jnp.where(jnp.arange(N_HEAD * NEW_COL) == chosen_row, PRE, values)
    return values.reshape(N_HEAD, NEW_COL).astype(jnp.int32)


def block_levels(rng, extent, shards, least, high):
    def one(dim, blocks):
        steps = jax.random.uniform(jax.random.fold_in(jax.random.fold_in(rng, 6), dim), (blocks,), jnp.float32, least / len(shards), high / len(shards))
        return jnp.repeat(jnp.exp(steps), extent[dim] // blocks).reshape((-1,) + (1,) * (len(extent) - dim - 1))

    factor_of = one(*shards[0])
    for cut in shards[1:]:
        factor_of = factor_of * one(*cut)
    return factor_of


def deal_out(key, own, number, rows, count, top, bound, lean):
    sequence = jax.random.permutation(key, count)
    crowded, usual = portions_of(count, rows * top, bound, lean, True), portions_of(count, rows * top, bound, lean, False)
    places = jnp.arange(count)

    def named(tallies, offset_by):
        used = int((tallies > 0).sum())
        fixed = max(1, used // 4)
        moved = fixed + (places - fixed + offset_by * (used - fixed)) % max(1, count - fixed)
        return jnp.zeros((count,), jnp.int32).at[sequence[jnp.where(places < fixed, places, moved)]].set(jnp.asarray(tallies, jnp.int32))

    tallies = jnp.where(number % 4 == 0, named(crowded, number // 4), named(usual, number - number // 4 - 1))
    mixed = jax.random.permutation(jax.random.fold_in(own, 3), count)
    source_of, receiver = mixed[0:count // 2 * 2:2], mixed[1:count // 2 * 2:2]
    margin = jnp.minimum(tallies[source_of] - 1, bound - tallies[receiver]) // 2
    margin = jnp.where((source_of == sequence[0]) | (receiver == sequence[0]) | (tallies[receiver] == 0), 0, jnp.maximum(margin, 0))
    moved = jax.random.randint(jax.random.fold_in(own, 4), (count // 2,), 0, 1 << 20) % (margin + 1)
    tallies = tallies.at[source_of].add(-moved).at[receiver].add(moved)
    items = jnp.searchsorted(jnp.cumsum(tallies), jnp.arange(rows * top), side="right").astype(jnp.int32)
    table = items.reshape(top, rows).T
    table = table[jax.random.permutation(jax.random.fold_in(own, 1), rows)]
    offset_by = jax.random.randint(jax.random.fold_in(own, 2), (rows, 1), 0, top)
    return jnp.take_along_axis(table, (jnp.arange(top)[None, :] + offset_by) % top, axis=1)


def portions_of(number_of, total, most, skew, full):
    loads = [(1 << 20) // math.isqrt(grade ** skew) + 1 for grade in range(1, number_of + 1)]
    largest = most if full else min(most, max(-(-total // number_of), total * loads[0] // sum(loads)))
    least = 1 if total - largest >= number_of - 1 else 0
    counts, rest = [largest] + [least] * (number_of - 1), total - largest - least * (number_of - 1)
    while rest > 0:
        movable = [i for i in range(1, number_of) if counts[i] < largest] or [i for i in range(1, number_of) if counts[i] < most]
        pool, budget = sum([loads[i] for i in movable]), rest
        for i in movable:
            extra = min(most - counts[i], max(1, budget * loads[i] // pool), rest)
            counts[i] = counts[i] + extra
            rest = rest - extra
    return np.array(counts)


def noise(key, dims, scale, limit, cuts=(), kind=jnp.bfloat16):
    level = block_levels(key, dims, cuts, -0.22, 0.18) if cuts else 1.0
    entries = jax.random.normal(key, dims, jnp.float32) * scale * level
    return jnp.minimum(jnp.maximum(entries, -limit), limit).astype(kind)


def setup_inputs(seed: int = 0) -> dict:
    key_of = jax.random.split(jax.random.key(seed), 16)
    hidden_in = noise(key_of[0], (STEPS, ROWS, D), 1.0, 6.0, ((1, 256),))
    queries = draw_queries(jax.random.fold_in(key_of[15], 71), 0)
    fresh = noise(key_of[2], (STEPS, ROWS, KD), 1.0, 6.0, ((1, 256),))
    res_cache = draw_res_cache(jax.random.fold_in(key_of[15], 71), 0)
    res_len = draw_res_len(jax.random.fold_in(key_of[15], 71), 0)
    pre_cache = draw_pre_cache(jax.random.fold_in(key_of[15], 71), 0)
    pre_len = draw_pre_len(jax.random.fold_in(key_of[15], 71), 0)
    arrival = jax.vmap(lambda own: jax.random.permutation(own, NEW_COL))(jax.random.split(key_of[7], N_HEAD)).reshape((N_HEAD, NEW_COL)).astype(jnp.int32)
    w_uv = noise(key_of[8], (HEADS, LAT, VD), LAT ** -0.5, 0.25, ((0, 16),))
    w_o = noise(key_of[9], (HEADS * VD, D), (HEADS * VD) ** -0.5, 0.0625, ((0, 16), (1, 16)))
    norm_gain = jnp.clip(1.0 + 0.1 * jax.random.normal(key_of[10], (D,), jnp.float32), 0.5, 1.5)
    expert_ids_keys = jax.random.split(jax.random.fold_in(key_of[11], 1), STEPS * ROWS // (ROWS_DEV * N_HEAD))
    expert_ids_turns = jax.random.permutation(jax.random.fold_in(key_of[11], 3), STEPS * ROWS // (ROWS_DEV * N_HEAD))
    expert_ids = jax.vmap(lambda own, number: deal_out(jax.random.fold_in(key_of[11], 2), own, number, ROWS_DEV * N_HEAD, EXPERTS, TOPK, CAP, 2))(expert_ids_keys, expert_ids_turns).reshape((STEPS, ROWS, TOPK))
    route_weight = jnp.clip(0.2 + 0.8 * jax.random.uniform(key_of[12], (STEPS, ROWS, TOPK), jnp.float32) ** block_levels(key_of[12], (STEPS, ROWS, TOPK), ((1, 16),), -0.2, 0.2), 0.2, 1.0)
    w_gu = noise(key_of[13], (EXP_WIN, 2, D, FFE), D ** -0.5, 0.0625, ((0, 16), (3, 16)))
    w_down = noise(key_of[14], (EXP_WIN, FFE, D), FFE ** -0.5, 0.125, ((0, 16), (2, 16)))
    return dict(hidden_in=hidden_in, queries=queries, fresh=fresh, res_cache=res_cache, res_len=res_len, pre_cache=pre_cache, pre_len=pre_len, arrival=arrival, w_uv=w_uv, w_o=w_o, norm_gain=norm_gain, expert_ids=expert_ids, route_weight=route_weight, w_gu=w_gu, w_down=w_down)


def attend(query_rows, key_rows, lengths, recent):
    scaling = (VD + ROPE) ** (-0.5)
    query_wide = query_rows.astype(jnp.float32)
    key_wide = key_rows.astype(jnp.float32)
    recent_wide = recent.astype(jnp.float32)
    cache_scores = jnp.einsum('nhk,npk->nhp', query_wide, key_wide) * scaling
    places = lax.broadcasted_iota(jnp.int32, (1, 1, key_rows.shape[1]), 2)
    cache_scores = jnp.where(places < lengths[:, None, None], cache_scores, -jnp.inf)
    fresh_scores = jnp.einsum('nhk,nsk->nhs', query_wide, recent_wide) * scaling
    highest = jnp.maximum(lax.optimization_barrier(jnp.max(cache_scores, axis=2)), lax.optimization_barrier(jnp.max(fresh_scores, axis=2)))[:, :, None]
    cache_weights = jnp.exp(cache_scores - highest)
    fresh_weights = jnp.exp(fresh_scores - highest)
    totals = lax.optimization_barrier(jnp.sum(cache_weights, axis=2, keepdims=True)) + lax.optimization_barrier(jnp.sum(fresh_weights, axis=2, keepdims=True))
    cache_probs = lax.optimization_barrier((cache_weights / totals).astype(jnp.bfloat16)).astype(jnp.float32)
    fresh_probs = lax.optimization_barrier((fresh_weights / totals).astype(jnp.bfloat16)).astype(jnp.float32)
    context = jnp.einsum('nhp,npl->nhl', cache_probs, key_wide[:, :, :LAT])
    context = context + jnp.einsum('nhs,nsl->nhl', fresh_probs, recent_wide[:, :, :LAT])
    return context.astype(jnp.bfloat16)

def single(operands):
    query_rows, key_rows, lengths, recent = operands
    return attend(query_rows[None], key_rows[None], lengths[None], recent[None])[0]

def routing(ids_rows, weights_rows, expert):
    matched = ids_rows == expert
    present = jnp.any(matched, axis=1).astype(jnp.int32)
    row_weight = lax.optimization_barrier(jnp.sum(jnp.where(matched, weights_rows, jnp.zeros_like(weights_rows)), axis=1))
    slot_index = jnp.cumsum(present) - present
    chosen = (slot_index[None, :] == jnp.arange(CAP, dtype=jnp.int32)[:, None]) & (present[None, :] == 1)
    return (chosen.astype(jnp.float32), row_weight)

def reference(hidden_in, queries, fresh, res_cache, res_len, pre_cache, pre_len, arrival, w_uv, w_o, norm_gain, expert_ids, route_weight, w_gu, w_down):
    devices = N_GROUP * N_HEAD
    owner_slot = jnp.argsort(arrival, axis=1).astype(jnp.int32)
    new_cache = jax.vmap(lambda column, picks: jnp.take(column, picks, axis=0))(pre_cache, owner_slot)
    new_len = jax.vmap(lambda column, picks: jnp.take(column, picks, axis=0))(pre_len, owner_slot)
    new_cache = new_cache.reshape(N_HEAD, N_GROUP, NEW_DEV, PRE, KD).transpose(1, 0, 2, 3, 4).reshape(devices * NEW_DEV, PRE, KD)
    new_len = new_len.reshape(N_HEAD, N_GROUP, NEW_DEV).transpose(1, 0, 2).reshape(devices * NEW_DEV).astype(jnp.int32)
    group_rows = ROWS_DEV * N_HEAD
    layer_rows = []
    for step_index in range(STEPS):
        recent = jnp.swapaxes(fresh[:step_index + 1], 0, 1).reshape(devices, ROWS_DEV, step_index + 1, KD)
        asked_rows = queries[step_index].reshape(devices, ROWS_DEV, HEADS, KD)
        resident_part = lax.map(single, (asked_rows[:, :R_DEV].reshape(-1, HEADS, KD), res_cache, res_len, recent[:, :R_DEV].reshape(-1, step_index + 1, KD)))
        arrived_part = lax.map(single, (asked_rows[:, R_DEV:].reshape(-1, HEADS, KD), new_cache, new_len, recent[:, R_DEV:].reshape(-1, step_index + 1, KD)))
        context = jnp.concatenate([resident_part.reshape(devices, R_DEV, HEADS, LAT), arrived_part.reshape(devices, NEW_DEV, HEADS, LAT)], axis=1).reshape(ROWS, HEADS, LAT)
        values = jnp.einsum('rhl,hlv->rhv', context.astype(jnp.float32), w_uv.astype(jnp.float32)).astype(jnp.bfloat16).reshape(ROWS, HEADS * VD)
        attention = jnp.dot(values, w_o, preferred_element_type=jnp.float32)
        summed = hidden_in[step_index].astype(jnp.float32) + attention
        normed = (summed * lax.rsqrt(lax.optimization_barrier(jnp.mean(summed * summed, axis=1, keepdims=True)) + 1e-06) * norm_gain.astype(jnp.float32)).astype(jnp.bfloat16)
        group_tokens = normed.reshape(N_GROUP, group_rows, D).astype(jnp.float32)
        ids_groups = expert_ids[step_index].reshape(N_GROUP, group_rows, TOPK)
        weights_groups = route_weight[step_index].reshape(N_GROUP, group_rows, TOPK)

        def one_expert(running, expert):
            packers, row_weights = jax.vmap(routing, in_axes=(0, 0, None))(ids_groups, weights_groups, expert)
            packed = jnp.einsum('gcr,grd->gcd', packers, group_tokens, precision=lax.Precision.HIGHEST).astype(jnp.bfloat16).reshape(N_GROUP * CAP, D)
            gate_part = jnp.dot(packed, w_gu[expert, 0], preferred_element_type=jnp.float32)
            up_part = jnp.dot(packed, w_gu[expert, 1], preferred_element_type=jnp.float32)
            active = (jax.nn.silu(gate_part) * up_part).astype(jnp.bfloat16)
            outcome = jnp.dot(active, w_down[expert], preferred_element_type=jnp.float32).reshape(N_GROUP, CAP, D)
            spread = packers * row_weights[:, None, :]
            return (running + jnp.einsum('gcr,gcd->grd', spread, outcome, precision=lax.Precision.HIGHEST), None)
        expert_mix, _ = lax.scan(one_expert, jnp.zeros((N_GROUP, group_rows, D), jnp.float32), jnp.arange(EXP_WIN, dtype=jnp.int32))
        layer_rows.append((summed + expert_mix.reshape(ROWS, D)).astype(jnp.bfloat16))
    return jnp.stack(layer_rows)
```

```python
import jax
import jax.numpy as jnp
from jax import lax
from jax.experimental import pallas as pl
from jax.experimental.pallas import tpu as pltpu
from jax.sharding import PartitionSpec as P

LAT = 512
ROPE = 64
VD = 128
CAP = 4
STEPS = 2


def attend(query_rows, key_rows, lengths, recent):
    rows, steps, heads, width = query_rows.shape
    scaling = (VD + ROPE) ** (-0.5)
    flat = query_rows.reshape(rows, steps * heads, width)
    cache_scores = (
        jnp.einsum("nqk,npk->nqp", flat, key_rows, preferred_element_type=jnp.float32) * scaling
    )
    places = lax.broadcasted_iota(jnp.int32, (1, 1, key_rows.shape[1]), 2)
    cache_scores = jnp.where(places < lengths[:, None, None], cache_scores, -jnp.inf)
    fresh_scores = (
        jnp.einsum("nqk,nsk->nqs", flat, recent, preferred_element_type=jnp.float32) * scaling
    )
    step_of = jnp.arange(steps * heads, dtype=jnp.int32)[:, None] // heads
    seen = jnp.arange(steps, dtype=jnp.int32)[None, :] <= step_of
    fresh_scores = jnp.where(seen[None], fresh_scores, -jnp.inf)
    highest = jnp.maximum(jnp.max(cache_scores, axis=2), jnp.max(fresh_scores, axis=2))[:, :, None]
    cache_weights = jnp.exp(cache_scores - highest)
    fresh_weights = jnp.exp(fresh_scores - highest)
    totals = jnp.sum(cache_weights, axis=2, keepdims=True) + jnp.sum(
        fresh_weights, axis=2, keepdims=True
    )
    cache_probs = (cache_weights / totals).astype(jnp.bfloat16)
    fresh_probs = (fresh_weights / totals).astype(jnp.bfloat16)
    context = jnp.einsum(
        "nqp,npl->nql", cache_probs, key_rows[:, :, :LAT], preferred_element_type=jnp.float32
    )
    context = context + jnp.einsum(
        "nqs,nsl->nql", fresh_probs, recent[:, :, :LAT], preferred_element_type=jnp.float32
    )
    return context.astype(jnp.bfloat16).reshape(rows, steps, heads, LAT)


def routing(ids, weights, experts):
    matched = ids[None] == jnp.arange(experts, dtype=jnp.int32)[:, None, None, None]
    present = jnp.any(matched, axis=3)
    row_weight = jnp.sum(jnp.where(matched, weights[None], 0.0), axis=3)
    rows = ids.shape[1]
    before = (
        jnp.arange(rows, dtype=jnp.int32)[:, None] < jnp.arange(rows, dtype=jnp.int32)[None, :]
    )
    slot_index = jnp.einsum(
        "etr,rs->ets",
        present.astype(jnp.bfloat16),
        before.astype(jnp.bfloat16),
        preferred_element_type=jnp.float32,
    ).astype(jnp.int32)
    slots = jnp.arange(CAP, dtype=jnp.int32)[None, None, :, None]
    chosen = (slot_index[:, :, None, :] == slots) & present[:, :, None, :]
    return chosen, row_weight


def project_body(x_ref, w_ref, own_ref, hidden_ref, rows_ref, slots_ref):
    blocks, _, width = w_ref.shape
    half = x_ref.shape[0] // 2
    parts = [
        jnp.dot(x_ref[...], w_ref[b], preferred_element_type=jnp.float32) for b in range(blocks)
    ]
    whole = jnp.concatenate(parts, axis=1)
    rows_ref[...] = whole[:half].astype(jnp.bfloat16)
    carried = jnp.dot(own_ref[...], hidden_ref[...], preferred_element_type=jnp.float32)
    slots_ref[...] = (whole[half:] + carried).astype(jnp.bfloat16)


def project(x, w, own, hidden):
    blocks, depth, width = w.shape
    half = x.shape[0] // 2
    each = 4
    out = jax.ShapeDtypeStruct((half, blocks * width), jnp.bfloat16)
    return pl.pallas_call(
        project_body,
        grid=(blocks // each,),
        in_specs=[
            pl.BlockSpec(x.shape, lambda i: (0, 0)),
            pl.BlockSpec((each, depth, width), lambda i: (i, 0, 0)),
            pl.BlockSpec(own.shape, lambda i: (0, 0)),
            pl.BlockSpec((hidden.shape[0], each * width), lambda i: (0, i)),
        ],
        out_specs=[pl.BlockSpec((half, each * width), lambda i: (0, i))] * 2,
        out_shape=[out, out],
        compiler_params=pltpu.CompilerParams(vmem_limit_bytes=40 * 1024 * 1024),
        cost_estimate=pl.CostEstimate(
            flops=2 * x.shape[0] * blocks * depth * width,
            bytes_accessed=2 * blocks * depth * width + 4 * x.shape[0] * blocks * width,
            transcendentals=0,
        ),
        name="project",
    )(x, w, own, hidden)


def per_device(
    hidden_in,
    queries,
    fresh,
    res_cache,
    res_len,
    pre_cache,
    pre_len,
    arrival,
    w_uv,
    w_o,
    norm_gain,
    expert_ids,
    route_weight,
    w_gu,
    w_down,
):
    groups = lax.axis_size("group")
    columns = lax.axis_size("head")
    group_index = lax.axis_index("group")
    head_index = lax.axis_index("head")
    steps, rows_dev, width = hidden_in.shape
    resident = res_cache.shape[0]
    newcomers = rows_dev - resident
    requests = arrival.shape[1]
    own_rows = steps * rows_dev
    rows_group = columns * own_rows
    heads_dev = w_uv.shape[0]
    slots_dev = steps * CAP

    w_all = lax.all_gather(w_o, "group", axis=0, tiled=False)

    places = jnp.arange(requests, dtype=jnp.int32)
    arrival_row = arrival[0]
    claimed = arrival_row[None, :] == places[:, None]
    order = jnp.sum(jnp.where(claimed, places[None, :], 0), axis=1)
    len_sorted = jnp.sum(jnp.where(claimed, pre_len[0][None, :], 0), axis=1)
    new_len = lax.dynamic_slice(len_sorted, (group_index * newcomers,), (newcomers,))
    sorted_cache = jnp.take(pre_cache[0], order, axis=0)
    taken = lax.all_to_all(
        sorted_cache.reshape(groups, newcomers, *sorted_cache.shape[1:]),
        "group",
        split_axis=0,
        concat_axis=0,
        tiled=False,
    )
    taken = jnp.swapaxes(taken, 0, 1).reshape(newcomers, -1, sorted_cache.shape[2])

    chosen, row_weight = routing(expert_ids, route_weight, columns)
    by_row = chosen.reshape(columns, steps, CAP, columns, rows_dev)
    same = jnp.arange(steps)[:, None] == jnp.arange(steps)[None, :]
    chooser = by_row[:, :, :, :, None, :] & same[None, :, None, None, :, None]
    chooser = chooser.reshape(columns * slots_dev, rows_group).astype(jnp.bfloat16)
    own_chooser = lax.dynamic_slice(
        chooser, (0, head_index * own_rows), (columns * slots_dev, own_rows)
    )
    mine = lax.dynamic_slice(chooser, (head_index * slots_dev, 0), (slots_dev, rows_group))
    weight_mine = lax.dynamic_slice(
        row_weight, (head_index, 0, 0), (1, steps, columns * rows_dev)
    )[0]
    weight_mine = jnp.swapaxes(weight_mine.reshape(steps, columns, rows_dev), 0, 1).reshape(
        rows_group, 1
    )
    spread = mine.astype(jnp.float32).T * weight_mine

    by_row_queries = jnp.swapaxes(queries, 0, 1)
    recent = jnp.swapaxes(fresh, 0, 1)
    context = jnp.concatenate(
        [
            attend(by_row_queries[:resident], res_cache, res_len, recent[:resident]),
            attend(by_row_queries[resident:], taken, new_len, recent[resident:]),
        ],
        axis=0,
    )
    context = context.reshape(rows_dev, steps, columns, heads_dev, LAT).transpose(2, 3, 1, 0, 4)
    by_head = lax.all_to_all(context, "head", split_axis=0, concat_axis=0, tiled=False)
    by_head = jnp.swapaxes(by_head, 0, 1).reshape(heads_dev, rows_group, LAT)
    values = jnp.einsum("hrl,hlv->rhv", by_head, w_uv, preferred_element_type=jnp.float32).astype(
        jnp.bfloat16
    )
    values = values.reshape(rows_group, heads_dev * VD)
    values_slots = jnp.dot(chooser, values, preferred_element_type=jnp.float32).astype(jnp.bfloat16)
    hidden_own = hidden_in.reshape(own_rows, width)
    part_rows, part_slots = project(
        jnp.concatenate([values, values_slots], axis=0), w_all, own_chooser, hidden_own
    )

    slot_parts = lax.all_to_all(
        part_slots.reshape(columns, slots_dev, width), "head", 0, 0, tiled=False
    )
    slot_rows = jnp.sum(slot_parts.astype(jnp.float32), axis=0)
    normed = (
        slot_rows
        * lax.rsqrt(jnp.mean(slot_rows * slot_rows, axis=1, keepdims=True) + 1e-06)
        * norm_gain
    ).astype(jnp.bfloat16)
    portion = lax.all_gather(normed, "group", axis=0, tiled=True)

    row_parts = lax.all_to_all(
        part_rows.reshape(columns, own_rows, width), "head", 0, 0, tiled=False
    )
    summed = hidden_own.astype(jnp.float32) + jnp.sum(row_parts.astype(jnp.float32), axis=0)

    gate_part = jnp.dot(portion, w_gu[0, 0], preferred_element_type=jnp.float32)
    up_part = jnp.dot(portion, w_gu[0, 1], preferred_element_type=jnp.float32)
    active = (jax.nn.silu(gate_part) * up_part).astype(jnp.bfloat16)
    outcome = jnp.dot(
        lax.all_gather(active, "group", axis=1, tiled=True),
        w_down[0],
        preferred_element_type=jnp.float32,
    )
    slot_values = lax.all_to_all(
        outcome.reshape(groups, slots_dev, outcome.shape[1]).astype(jnp.bfloat16),
        "group",
        split_axis=0,
        concat_axis=2,
        tiled=True,
    ).reshape(slots_dev, width)
    mixed = jnp.dot(
        spread,
        slot_values.astype(jnp.float32),
        precision=lax.Precision.HIGHEST,
        preferred_element_type=jnp.float32,
    ).astype(jnp.bfloat16)
    mix_parts = lax.all_to_all(mixed.reshape(columns, own_rows, width), "head", 0, 0, tiled=False)
    out = summed + jnp.sum(mix_parts.astype(jnp.float32), axis=0)
    return out.astype(jnp.bfloat16).reshape(steps, rows_dev, width)


def solution(mesh):
    placed = (
        P(None, ("group", "head"), None),
        P(None, ("group", "head"), None, None),
        P(None, ("group", "head"), None),
        P(("group", "head"), None, None),
        P(("group", "head")),
        P("head", None, "group", None),
        P("head", None),
        P("head", None),
        P("head", None, None),
        P("head", "group"),
        P(),
        P(None, "group", None),
        P(None, "group", None),
        P("head", None, None, "group"),
        P("head", None, "group"),
    )
    return jax.shard_map(
        per_device,
        mesh=mesh,
        in_specs=placed,
        out_specs=P(None, ("group", "head"), None),
        check_vma=False,
    )
```

```python
import jax
import jax.numpy as jnp
from jax import lax
from jax.experimental import pallas as pl
from jax.experimental.pallas import tpu as pltpu
from jax.sharding import Mesh
from jax.sharding import PartitionSpec as P

LAT = 512
ROPE = 64
VD = 128
CAP = 4
STEPS = 2


def attend(query_rows, key_rows, lengths, recent):
    rows, steps, heads, width = query_rows.shape
    scaling = (VD + ROPE) ** (-0.5)
    flat = query_rows.reshape(rows, steps * heads, width)
    cache_scores = (
        jnp.einsum("nqk,npk->nqp", flat, key_rows, preferred_element_type=jnp.float32) * scaling
    )
    places = lax.broadcasted_iota(jnp.int32, (1, 1, key_rows.shape[1]), 2)
    cache_scores = jnp.where(places < lengths[:, None, None], cache_scores, -jnp.inf)
    fresh_scores = (
        jnp.einsum("nqk,nsk->nqs", flat, recent, preferred_element_type=jnp.float32) * scaling
    )
    step_of = jnp.arange(steps * heads, dtype=jnp.int32)[:, None] // heads
    seen = jnp.arange(steps, dtype=jnp.int32)[None, :] <= step_of
    fresh_scores = jnp.where(seen[None], fresh_scores, -jnp.inf)
    highest = jnp.maximum(jnp.max(cache_scores, axis=2), jnp.max(fresh_scores, axis=2))[:, :, None]
    cache_weights = jnp.exp(cache_scores - highest)
    fresh_weights = jnp.exp(fresh_scores - highest)
    totals = jnp.sum(cache_weights, axis=2, keepdims=True) + jnp.sum(
        fresh_weights, axis=2, keepdims=True
    )
    cache_probs = (cache_weights / totals).astype(jnp.bfloat16)
    fresh_probs = (fresh_weights / totals).astype(jnp.bfloat16)
    context = jnp.einsum(
        "nqp,npl->nql", cache_probs, key_rows[:, :, :LAT], preferred_element_type=jnp.float32
    )
    context = context + jnp.einsum(
        "nqs,nsl->nql", fresh_probs, recent[:, :, :LAT], preferred_element_type=jnp.float32
    )
    return context.astype(jnp.bfloat16).reshape(rows, steps, heads, LAT)


def routing(ids, weights, experts):
    matched = ids[None] == jnp.arange(experts, dtype=jnp.int32)[:, None, None, None]
    present = jnp.any(matched, axis=3)
    row_weight = jnp.sum(jnp.where(matched, weights[None], 0.0), axis=3)
    rows = ids.shape[1]
    before = (
        jnp.arange(rows, dtype=jnp.int32)[:, None] < jnp.arange(rows, dtype=jnp.int32)[None, :]
    )
    slot_index = jnp.einsum(
        "etr,rs->ets",
        present.astype(jnp.bfloat16),
        before.astype(jnp.bfloat16),
        preferred_element_type=jnp.float32,
    ).astype(jnp.int32)
    slots = jnp.arange(CAP, dtype=jnp.int32)[None, None, :, None]
    chosen = (slot_index[:, :, None, :] == slots) & present[:, :, None, :]
    return chosen, row_weight


def project_body(x_ref, w_ref, own_ref, hidden_ref, rows_ref, slots_ref):
    half = x_ref.shape[0] // 2
    whole = lax.dot_general(
        x_ref[...], w_ref[...], (((1,), (1,)), ((), ())), preferred_element_type=jnp.float32
    )
    rows_ref[...] = whole[:half].reshape(rows_ref.shape)
    carried = jnp.dot(own_ref[...], hidden_ref[...], preferred_element_type=jnp.float32)
    slots_ref[...] = (whole[half:] + carried).astype(jnp.bfloat16)


def project(x, w, own, hidden):
    width, depth = w.shape
    half = x.shape[0] // 2
    tile = width // 8
    each = hidden.shape[0]
    return pl.pallas_call(
        project_body,
        grid=(width // tile,),
        in_specs=[
            pl.BlockSpec(x.shape, lambda i: (0, 0)),
            pl.BlockSpec((tile, depth), lambda i: (i, 0)),
            pl.BlockSpec(own.shape, lambda i: (0, 0)),
            pl.BlockSpec((hidden.shape[0], tile), lambda i: (0, i)),
        ],
        out_specs=[
            pl.BlockSpec((half // each, 1, each, tile), lambda i: (0, i, 0, 0)),
            pl.BlockSpec((half, tile), lambda i: (0, i)),
        ],
        out_shape=[
            jax.ShapeDtypeStruct((half // each, width // tile, each, tile), jnp.float32),
            jax.ShapeDtypeStruct((half, width), jnp.bfloat16),
        ],
        compiler_params=pltpu.CompilerParams(vmem_limit_bytes=40 * 1024 * 1024),
        cost_estimate=pl.CostEstimate(
            flops=2 * x.shape[0] * depth * width,
            bytes_accessed=2 * depth * width + 4 * x.shape[0] * width,
            transcendentals=0,
        ),
        name="project",
    )(x, w, own, hidden)


def gate_up_body(x_ref, own_ref, other_ref, active_ref, gate, up):
    step = pl.program_id(0)

    @pl.when(step == 0)
    def _():
        gate[...] = jnp.zeros_like(gate)
        up[...] = jnp.zeros_like(up)

    x = x_ref[...]
    for part, total in ((0, gate), (1, up)):
        both = jnp.concatenate([own_ref[part], other_ref[part]], axis=1)
        total[...] += jnp.dot(x, both, preferred_element_type=jnp.float32)

    @pl.when(step == pl.num_programs(0) - 1)
    def _():
        g = gate[...]
        active_ref[...] = (g * jax.nn.sigmoid(g) * up[...]).astype(jnp.bfloat16)


def gate_up(x, own, other):
    rows, depth = x.shape
    units = own.shape[2]
    tile = depth // 7
    return pl.pallas_call(
        gate_up_body,
        grid=(depth // tile,),
        in_specs=[
            pl.BlockSpec((rows, tile), lambda i: (0, i)),
            pl.BlockSpec((2, tile, units), lambda i: (0, i, 0)),
            pl.BlockSpec((2, tile, units), lambda i: (0, i, 0)),
        ],
        out_specs=pl.BlockSpec((rows, 2 * units), lambda i: (0, 0)),
        out_shape=jax.ShapeDtypeStruct((rows, 2 * units), jnp.bfloat16),
        scratch_shapes=[pltpu.VMEM((rows, 2 * units), jnp.float32)] * 2,
        compiler_params=pltpu.CompilerParams(vmem_limit_bytes=24 * 1024 * 1024),
        cost_estimate=pl.CostEstimate(
            flops=8 * rows * depth * units,
            bytes_accessed=8 * depth * units + 2 * rows * depth,
            transcendentals=2 * rows * units,
        ),
        name="gate_up",
    )(x, own, other)


def swap_cores(x):
    return lax.ppermute(x, "core", [(0, 1), (1, 0)])


def per_device(
    hidden_in,
    queries,
    fresh,
    res_cache,
    res_len,
    pre_cache,
    pre_len,
    arrival,
    w_uv,
    w_o,
    norm_gain,
    expert_ids,
    route_weight,
    w_gu,
    w_down,
):
    group, head = ("z", "core"), ("y", "x")
    chips, cores, long, short = (lax.axis_size(a) for a in ("z", "core", "y", "x"))
    groups, columns = chips * cores, long * short
    core, at_y, at_x = (lax.axis_index(a) for a in ("core", "y", "x"))
    group_index = lax.axis_index(group)
    head_index = lax.axis_index(head)
    steps, rows_dev, width = hidden_in.shape
    resident = res_cache.shape[0]
    newcomers = rows_dev - resident
    requests = arrival.shape[1]
    own_rows = steps * rows_dev
    rows_group = columns * own_rows
    heads_dev = w_uv.shape[0]
    slots_dev = steps * CAP

    w_all = lax.all_gather(w_o.T, group, axis=0, tiled=True)
    gu_other = swap_cores(w_gu[0])
    down = w_down[0].T
    down_other = swap_cores(down)

    places = jnp.arange(requests, dtype=jnp.int32)
    arrival_row = arrival[0]
    claimed = arrival_row[None, :] == places[:, None]
    order = jnp.sum(jnp.where(claimed, places[None, :], 0), axis=1)
    len_sorted = jnp.sum(jnp.where(claimed, pre_len[0][None, :], 0), axis=1)
    new_len = lax.dynamic_slice(len_sorted, (group_index * newcomers,), (newcomers,))
    sorted_cache = jnp.take(pre_cache[0], order, axis=0, mode="clip")
    taken = lax.all_to_all(
        sorted_cache.reshape(groups, newcomers, *sorted_cache.shape[1:]),
        group,
        split_axis=0,
        concat_axis=0,
        tiled=False,
    )
    taken = jnp.swapaxes(taken, 0, 1).reshape(newcomers, -1, sorted_cache.shape[2])

    chosen, row_weight = routing(expert_ids, route_weight, columns)
    by_row = chosen.reshape(columns, steps, CAP, columns, rows_dev)
    same = jnp.arange(steps)[:, None] == jnp.arange(steps)[None, :]
    chooser = by_row[:, :, :, :, None, :] & same[None, :, None, None, :, None]
    chooser = chooser.reshape(columns * slots_dev, rows_group).astype(jnp.bfloat16)
    own_chooser = lax.dynamic_slice(
        chooser, (0, head_index * own_rows), (columns * slots_dev, own_rows)
    )
    near = jnp.where(chosen, row_weight[:, :, None, :], 0.0).reshape(
        long, short, steps, CAP, long, short, rows_dev
    )
    near = lax.dynamic_index_in_dim(near, at_y, 0, keepdims=False)
    near = lax.dynamic_index_in_dim(near, at_x, 4, keepdims=False)
    spread = jnp.where(
        same[None, :, None, None, :, None], near[:, :, :, :, None, :], 0.0
    ).reshape(short * slots_dev, long * own_rows)

    by_row_queries = jnp.swapaxes(queries, 0, 1)
    recent = jnp.swapaxes(fresh, 0, 1)
    context = jnp.concatenate(
        [
            attend(by_row_queries[:resident], res_cache, res_len, recent[:resident]),
            attend(by_row_queries[resident:], taken, new_len, recent[resident:]),
        ],
        axis=0,
    )
    context = context.reshape(rows_dev, steps, columns, heads_dev, LAT).transpose(2, 3, 1, 0, 4)
    by_head = lax.all_to_all(context, head, split_axis=0, concat_axis=0, tiled=False)
    by_head = jnp.swapaxes(by_head, 0, 1).reshape(heads_dev, rows_group, LAT)
    values = jnp.einsum("hrl,hlv->rhv", by_head, w_uv, preferred_element_type=jnp.float32).astype(
        jnp.bfloat16
    )
    values = values.reshape(rows_group, heads_dev * VD)
    values_slots = jnp.dot(chooser, values, preferred_element_type=jnp.float32).astype(jnp.bfloat16)
    hidden_own = hidden_in.reshape(own_rows, width)
    part_rows, part_slots = project(
        jnp.concatenate([values, values_slots], axis=0), w_all, own_chooser, hidden_own
    )
    blocks, tile = part_rows.shape[1], part_rows.shape[3]
    attention = lax.psum_scatter(
        part_rows.reshape(-1, tile), head, scatter_dimension=0, tiled=True
    ).reshape(blocks, own_rows, tile)
    summed = hidden_own.astype(jnp.float32) + jnp.swapaxes(attention, 0, 1).reshape(own_rows, width)

    slot_parts = lax.all_to_all(
        part_slots.reshape(columns, slots_dev, width), head, 0, 0, tiled=False
    )
    slot_rows = jnp.sum(slot_parts.astype(jnp.float32), axis=0)
    normed = (
        slot_rows
        * lax.rsqrt(jnp.mean(slot_rows * slot_rows, axis=1, keepdims=True) + 1e-06)
        * norm_gain
    ).astype(jnp.bfloat16)
    portion = lax.all_gather(normed, "z", axis=0, tiled=True)
    active = gate_up(portion, w_gu[0], gu_other)
    units = active.shape[1] // 2
    active = jnp.where(
        core == 0,
        active,
        jnp.concatenate([active[:, units:], active[:, :units]], axis=1),
    )
    copies = jnp.broadcast_to(active[None], (chips, *active.shape))
    copies = lax.all_to_all(copies, "z", 0, 0, tiled=False)
    everywhere = jnp.swapaxes(copies, 0, 1).reshape(active.shape[0], -1)
    second = (((1,), (1,)), ((), ()))
    mine = lax.dot_general(everywhere, down, second, preferred_element_type=jnp.float32)
    others = lax.dot_general(everywhere, down_other, second, preferred_element_type=jnp.float32)
    mine, others = mine.astype(jnp.bfloat16), others.astype(jnp.bfloat16)
    outcome = jnp.where(
        core == 0,
        jnp.concatenate([mine, others], axis=1),
        jnp.concatenate([others, mine], axis=1),
    )
    slot_values = lax.all_to_all(
        outcome.reshape(chips, slots_dev, outcome.shape[1]), "z", 0, 0, tiled=False
    )
    slot_values = jnp.swapaxes(slot_values, 0, 1).reshape(slots_dev, width)
    beside = lax.all_gather(slot_values, "x", axis=0, tiled=True)
    mixed = lax.dot_general(
        spread,
        beside.astype(jnp.float32),
        (((0,), (0,)), ((), ())),
        precision=lax.Precision.HIGHEST,
        preferred_element_type=jnp.float32,
    ).astype(jnp.bfloat16)
    mix_parts = lax.all_to_all(mixed.reshape(long, own_rows, width), "y", 0, 0, tiled=False)
    out = summed + jnp.sum(mix_parts.astype(jnp.float32), axis=0)
    return out.astype(jnp.bfloat16).reshape(steps, rows_dev, width)


def solution(mesh):
    wide = Mesh(mesh.devices.reshape(8, 2, 4, 4), ("z", "core", "y", "x"))
    group, head = ("z", "core"), ("y", "x")
    both = group + head
    placed = (
        P(None, both, None),
        P(None, both, None, None),
        P(None, both, None),
        P(both, None, None),
        P(both),
        P(head, None, group, None),
        P(head, None),
        P(head, None),
        P(head, None, None),
        P(head, group),
        P(),
        P(None, group, None),
        P(None, group, None),
        P(head, None, None, group),
        P(head, None, group),
    )
    return jax.shard_map(
        per_device,
        mesh=wide,
        in_specs=placed,
        out_specs=P(None, both, None),
        check_vma=False,
    )
```

```python
import functools

import jax
import jax.numpy as jnp
from jax import lax
from jax.experimental import pallas as pl
from jax.experimental.pallas import tpu as pltpu
from jax.sharding import Mesh
from jax.sharding import PartitionSpec as P

LAT = 512
ROPE = 64
VD = 128
CAP = 4
STEPS = 2


def attend(query_rows, key_rows, lengths, recent):
    rows, steps, heads, width = query_rows.shape
    scaling = (VD + ROPE) ** (-0.5)
    flat = query_rows.reshape(rows, steps * heads, width)
    cache_scores = (
        jnp.einsum("nqk,npk->nqp", flat, key_rows, preferred_element_type=jnp.float32) * scaling
    )
    places = lax.broadcasted_iota(jnp.int32, (1, 1, key_rows.shape[1]), 2)
    cache_scores = jnp.where(places < lengths[:, None, None], cache_scores, -jnp.inf)
    fresh_scores = (
        jnp.einsum("nqk,nsk->nqs", flat, recent, preferred_element_type=jnp.float32) * scaling
    )
    step_of = jnp.arange(steps * heads, dtype=jnp.int32)[:, None] // heads
    seen = jnp.arange(steps, dtype=jnp.int32)[None, :] <= step_of
    fresh_scores = jnp.where(seen[None], fresh_scores, -jnp.inf)
    highest = jnp.maximum(jnp.max(cache_scores, axis=2), jnp.max(fresh_scores, axis=2))[:, :, None]
    cache_weights = jnp.exp(cache_scores - highest)
    fresh_weights = jnp.exp(fresh_scores - highest)
    totals = jnp.sum(cache_weights, axis=2, keepdims=True) + jnp.sum(
        fresh_weights, axis=2, keepdims=True
    )
    cache_probs = (cache_weights / totals).astype(jnp.bfloat16)
    fresh_probs = (fresh_weights / totals).astype(jnp.bfloat16)
    context = jnp.einsum(
        "nqp,npl->nql", cache_probs, key_rows[:, :, :LAT], preferred_element_type=jnp.float32
    )
    context = context + jnp.einsum(
        "nqs,nsl->nql", fresh_probs, recent[:, :, :LAT], preferred_element_type=jnp.float32
    )
    return context.astype(jnp.bfloat16).reshape(rows, steps, heads, LAT)


def routing(ids, weights, experts):
    matched = ids[None] == jnp.arange(experts, dtype=jnp.int32)[:, None, None, None]
    present = jnp.any(matched, axis=3)
    row_weight = jnp.sum(jnp.where(matched, weights[None], 0.0), axis=3)
    rows = ids.shape[1]
    before = (
        jnp.arange(rows, dtype=jnp.int32)[:, None] < jnp.arange(rows, dtype=jnp.int32)[None, :]
    )
    slot_index = jnp.einsum(
        "etr,rs->ets",
        present.astype(jnp.bfloat16),
        before.astype(jnp.bfloat16),
        preferred_element_type=jnp.float32,
    ).astype(jnp.int32)
    slots = jnp.arange(CAP, dtype=jnp.int32)[None, None, :, None]
    chosen = (slot_index[:, :, None, :] == slots) & present[:, :, None, :]
    return chosen, row_weight


NT = (((1,), (1,)), ((), ()))


def project_slots_body(x_ref, w_ref, own_ref, hidden_ref, out_ref):
    whole = lax.dot_general(x_ref[...], w_ref[...], NT, preferred_element_type=jnp.float32)
    carried = jnp.dot(own_ref[...], hidden_ref[...], preferred_element_type=jnp.float32)
    out_ref[...] = (whole + carried).astype(jnp.bfloat16)


def project_slots(x, w, own, hidden):
    width, depth = w.shape
    rows = x.shape[0]
    tile = width // 4
    return pl.pallas_call(
        project_slots_body,
        grid=(width // tile,),
        in_specs=[
            pl.BlockSpec(x.shape, lambda i: (0, 0)),
            pl.BlockSpec((tile, depth), lambda i: (i, 0)),
            pl.BlockSpec(own.shape, lambda i: (0, 0)),
            pl.BlockSpec((hidden.shape[0], tile), lambda i: (0, i)),
        ],
        out_specs=pl.BlockSpec((rows, tile), lambda i: (0, i)),
        out_shape=jax.ShapeDtypeStruct((rows, width), jnp.bfloat16),
        compiler_params=pltpu.CompilerParams(vmem_limit_bytes=56 * 1024 * 1024),
        cost_estimate=pl.CostEstimate(
            flops=2 * rows * depth * width,
            bytes_accessed=2 * depth * width + 2 * rows * width,
            transcendentals=0,
        ),
        name="project_slots",
    )(x, w, own, hidden)


def project_rows_body(outer, x_ref, w_ref, out_ref):
    whole = lax.dot_general(x_ref[...], w_ref[...], NT, preferred_element_type=jnp.float32)
    blocks, _, each, _ = out_ref.shape
    inner = blocks // outer
    for k in range(blocks):
        out_ref[k % inner * outer + k // inner, 0] = whole[k * each : (k + 1) * each]


def project_rows(x, w, each, outer):
    width, depth = w.shape
    rows = x.shape[0]
    tile = width // 8
    return pl.pallas_call(
        functools.partial(project_rows_body, outer),
        grid=(width // tile,),
        in_specs=[
            pl.BlockSpec(x.shape, lambda i: (0, 0)),
            pl.BlockSpec((tile, depth), lambda i: (i, 0)),
        ],
        out_specs=pl.BlockSpec((rows // each, 1, each, tile), lambda i: (0, i, 0, 0)),
        out_shape=jax.ShapeDtypeStruct((rows // each, width // tile, each, tile), jnp.float32),
        compiler_params=pltpu.CompilerParams(vmem_limit_bytes=56 * 1024 * 1024),
        cost_estimate=pl.CostEstimate(
            flops=2 * rows * depth * width,
            bytes_accessed=2 * depth * width + 4 * rows * width,
            transcendentals=0,
        ),
        name="project_rows",
    )(x, w)


def after_body(x_ref, other_ref, out_ref):
    del x_ref, other_ref, out_ref


def after(x, other):
    return pl.pallas_call(
        after_body,
        in_specs=[pl.BlockSpec(memory_space=pl.ANY)] * 2,
        out_specs=pl.BlockSpec(memory_space=pl.ANY),
        out_shape=jax.ShapeDtypeStruct(x.shape, x.dtype),
        input_output_aliases={0: 0},
        name="after",
    )(x, other)


def gate_up_body(core_ref, x_ref, own_ref, other_ref, active_ref, gate, up):
    step = pl.program_id(0)

    @pl.when(step == 0)
    def _():
        gate[...] = jnp.zeros_like(gate)
        up[...] = jnp.zeros_like(up)

    x = x_ref[...]
    for part, total in ((0, gate), (1, up)):
        both = jnp.concatenate([own_ref[part], other_ref[part]], axis=1)
        total[...] += jnp.dot(x, both, preferred_element_type=jnp.float32)

    @pl.when(step == pl.num_programs(0) - 1)
    def _():
        g = gate[...]
        active = (g * jax.nn.sigmoid(g) * up[...]).astype(jnp.bfloat16)
        units = active.shape[1] // 2
        first, second = active[:, :units], active[:, units:]

        @pl.when(core_ref[0] == 0)
        def _():
            for k in range(active_ref.shape[0]):
                active_ref[k, :, :units] = first
                active_ref[k, :, units:] = second

        @pl.when(core_ref[0] != 0)
        def _():
            for k in range(active_ref.shape[0]):
                active_ref[k, :, :units] = second
                active_ref[k, :, units:] = first


def gate_up(core, x, own, other, copies):
    rows, depth = x.shape
    units = own.shape[2]
    tile = depth // 4
    return pl.pallas_call(
        gate_up_body,
        grid=(depth // tile,),
        in_specs=[
            pl.BlockSpec(memory_space=pltpu.SMEM),
            pl.BlockSpec((rows, tile), lambda i: (0, i)),
            pl.BlockSpec((2, tile, units), lambda i: (0, i, 0)),
            pl.BlockSpec((2, tile, units), lambda i: (0, i, 0)),
        ],
        out_specs=pl.BlockSpec((copies, rows, 2 * units), lambda i: (0, 0, 0)),
        out_shape=jax.ShapeDtypeStruct((copies, rows, 2 * units), jnp.bfloat16),
        scratch_shapes=[pltpu.VMEM((rows, 2 * units), jnp.float32)] * 2,
        compiler_params=pltpu.CompilerParams(vmem_limit_bytes=24 * 1024 * 1024),
        cost_estimate=pl.CostEstimate(
            flops=8 * rows * depth * units,
            bytes_accessed=8 * depth * units + 2 * rows * depth,
            transcendentals=2 * rows * units,
        ),
        name="gate_up",
    )(core, x, own, other)


def down_body(core_ref, x_ref, own_ref, other_ref, out_ref):
    x = jnp.concatenate([x_ref[k] for k in range(x_ref.shape[0])], axis=1)
    half = own_ref.shape[0]
    parts, each = out_ref.shape[0], out_ref.shape[1]
    mine = lax.dot_general(x, own_ref[...], NT, preferred_element_type=jnp.float32)
    others = lax.dot_general(x, other_ref[...], NT, preferred_element_type=jnp.float32)

    def write(first, second):
        both = jnp.concatenate([first, second], axis=1).reshape(parts, each, 2 * half)
        out_ref[...] = both.astype(jnp.bfloat16)

    @pl.when(core_ref[0] == 0)
    def _():
        write(mine, others)

    @pl.when(core_ref[0] != 0)
    def _():
        write(others, mine)


def down_project(core, x, own, other):
    parts, rows, _ = x.shape
    columns = 2 * own.shape[0]
    vmem = pl.BlockSpec(memory_space=pltpu.VMEM)
    return pl.pallas_call(
        down_body,
        in_specs=[pl.BlockSpec(memory_space=pltpu.SMEM), vmem, vmem, vmem],
        out_specs=vmem,
        out_shape=jax.ShapeDtypeStruct((parts, rows // parts, columns), jnp.bfloat16),
        compiler_params=pltpu.CompilerParams(vmem_limit_bytes=24 * 1024 * 1024),
        cost_estimate=pl.CostEstimate(
            flops=2 * rows * own.shape[1] * columns,
            bytes_accessed=2 * own.shape[1] * columns,
            transcendentals=0,
        ),
        name="down_project",
    )(core, x, own, other)


def combine_body(spread_ref, *refs):
    blocks, out_ref = refs[:-1], refs[-1]
    weight = spread_ref[...]
    high = weight.astype(jnp.bfloat16)
    low = (weight - high.astype(jnp.float32)).astype(jnp.bfloat16)
    parts, _, width = blocks[0].shape
    for k in range(parts):
        slots = jnp.concatenate([b[k].astype(jnp.float32) for b in blocks], axis=0)
        slots = slots.astype(jnp.bfloat16)
        mixed = jnp.dot(high, slots, preferred_element_type=jnp.float32) + jnp.dot(
            low, slots, preferred_element_type=jnp.float32
        )
        mixed = mixed.astype(jnp.bfloat16).reshape(*out_ref.shape[:2], width)
        out_ref[:, :, k * width : (k + 1) * width] = mixed


def combine(spread, blocks, each):
    rows = spread.shape[0]
    width = blocks[0].shape[0] * blocks[0].shape[2]
    vmem = pl.BlockSpec(memory_space=pltpu.VMEM)
    return pl.pallas_call(
        combine_body,
        in_specs=[vmem] * (1 + len(blocks)),
        out_specs=vmem,
        out_shape=jax.ShapeDtypeStruct((rows // each, each, width), jnp.bfloat16),
        compiler_params=pltpu.CompilerParams(vmem_limit_bytes=16 * 1024 * 1024),
        cost_estimate=pl.CostEstimate(
            flops=4 * rows * spread.shape[1] * width,
            bytes_accessed=2 * (rows + spread.shape[1]) * width,
            transcendentals=0,
        ),
        name="combine",
    )(spread, *blocks)


def shifted(x, axis, by):
    size = lax.axis_size(axis)
    return lax.ppermute(x, axis, [(i, (i + by) % size) for i in range(size)])


def swap_cores(x):
    return lax.ppermute(x, "core", [(0, 1), (1, 0)])


def per_device(
    hidden_in,
    queries,
    fresh,
    res_cache,
    res_len,
    pre_cache,
    pre_len,
    arrival,
    w_uv,
    w_o,
    norm_gain,
    expert_ids,
    route_weight,
    w_gu,
    w_down,
):
    group, head = ("z", "core"), ("y", "x")
    chips, cores, long, short = (lax.axis_size(a) for a in ("z", "core", "y", "x"))
    groups, columns = chips * cores, long * short
    core, at_y, at_x = (lax.axis_index(a) for a in ("core", "y", "x"))
    group_index = lax.axis_index(group)
    head_index = lax.axis_index(head)
    steps, rows_dev, width = hidden_in.shape
    resident = res_cache.shape[0]
    newcomers = rows_dev - resident
    requests = arrival.shape[1]
    own_rows = steps * rows_dev
    rows_group = columns * own_rows
    heads_dev = w_uv.shape[0]
    slots_dev = steps * CAP

    w_all = lax.all_gather(w_o.T, group, axis=0, tiled=True)
    gu_other = swap_cores(w_gu[0])
    down = w_down[0].T
    down_other = swap_cores(down)

    places = jnp.arange(requests, dtype=jnp.int32)
    arrival_row = arrival[0]
    claimed = arrival_row[None, :] == places[:, None]
    order = jnp.sum(jnp.where(claimed, places[None, :], 0), axis=1)
    len_sorted = jnp.sum(jnp.where(claimed, pre_len[0][None, :], 0), axis=1)
    new_len = lax.dynamic_slice(len_sorted, (group_index * newcomers,), (newcomers,))
    sorted_cache = jnp.take(pre_cache[0], order, axis=0, mode="clip")
    taken = lax.all_to_all(
        sorted_cache.reshape(groups, newcomers, *sorted_cache.shape[1:]),
        group,
        split_axis=0,
        concat_axis=0,
        tiled=False,
    )
    taken = jnp.swapaxes(taken, 0, 1).reshape(newcomers, -1, sorted_cache.shape[2])

    chosen, row_weight = routing(expert_ids, route_weight, columns)
    by_row = chosen.reshape(columns, steps, CAP, columns, rows_dev)
    same = jnp.arange(steps)[:, None] == jnp.arange(steps)[None, :]
    chooser = by_row[:, :, :, :, None, :] & same[None, :, None, None, :, None]
    chooser = chooser.reshape(columns * slots_dev, rows_group).astype(jnp.bfloat16)
    own_chooser = lax.dynamic_slice(
        chooser, (0, head_index * own_rows), (columns * slots_dev, own_rows)
    )
    near = jnp.where(chosen, row_weight[:, :, None, :], 0.0)
    expert_of = at_y * short + (at_x - jnp.arange(short, dtype=jnp.int32)) % short
    row_of = ((at_y + jnp.arange(long, dtype=jnp.int32)) % long * short + at_x) * rows_dev
    row_of = (row_of[:, None] + jnp.arange(rows_dev, dtype=jnp.int32)[None, :]).reshape(-1)
    pick_expert = expert_of[:, None] == jnp.arange(columns, dtype=jnp.int32)[None, :]
    pick_row = row_of[:, None] == jnp.arange(columns * rows_dev, dtype=jnp.int32)[None, :]
    exact = dict(precision=lax.Precision.HIGHEST, preferred_element_type=jnp.float32)
    near = jnp.einsum("je,etcr->jtcr", pick_expert.astype(jnp.float32), near, **exact)
    near = jnp.einsum("jtcr,qr->jtcq", near, pick_row.astype(jnp.float32), **exact)
    near = near.reshape(short, steps, CAP, long, rows_dev).transpose(3, 4, 0, 1, 2)
    spread = jnp.where(same[None, :, None, None, :, None], near[:, None], 0.0)
    spread = spread.reshape(long * own_rows, short * slots_dev)

    by_row_queries = jnp.swapaxes(queries, 0, 1)
    recent = jnp.swapaxes(fresh, 0, 1)
    context = jnp.concatenate(
        [
            attend(by_row_queries[:resident], res_cache, res_len, recent[:resident]),
            attend(by_row_queries[resident:], taken, new_len, recent[resident:]),
        ],
        axis=0,
    )
    context = context.reshape(rows_dev, steps, columns, heads_dev, LAT).transpose(2, 3, 1, 0, 4)
    by_head = lax.all_to_all(context, head, split_axis=0, concat_axis=0, tiled=False)
    by_head = jnp.swapaxes(by_head, 0, 1).reshape(heads_dev, rows_group, LAT)
    values = jnp.einsum("hrl,hlv->rhv", by_head, w_uv, preferred_element_type=jnp.float32).astype(
        jnp.bfloat16
    )
    values = values.reshape(rows_group, heads_dev * VD)
    values_slots = jnp.dot(chooser, values, preferred_element_type=jnp.float32).astype(jnp.bfloat16)
    hidden_own = hidden_in.reshape(own_rows, width)
    part_slots = project_slots(values_slots, w_all, own_chooser, hidden_own)
    slot_parts = lax.all_to_all(
        part_slots.reshape(columns, slots_dev, width), head, 0, 0, tiled=False
    )
    part_rows = project_rows(values, w_all, own_rows, long)
    slot_rows = jnp.sum(slot_parts.astype(jnp.float32), axis=0)
    normed = (
        slot_rows
        * lax.rsqrt(jnp.mean(slot_rows * slot_rows, axis=1, keepdims=True) + 1e-06)
        * norm_gain
    ).astype(jnp.bfloat16)

    blocks, tile = part_rows.shape[1], part_rows.shape[3]
    part_rows = after(part_rows.reshape(-1, tile), normed)
    part_rows = lax.psum_scatter(part_rows, "x", scatter_dimension=0, tiled=True)
    attention = lax.psum_scatter(part_rows, "y", scatter_dimension=0, tiled=True)
    attention = jnp.swapaxes(attention.reshape(blocks, own_rows, tile), 0, 1)
    summed = hidden_own.astype(jnp.float32) + attention.reshape(own_rows, width)

    core_now = jnp.reshape(core, (1,)).astype(jnp.int32)
    portion = lax.all_gather(normed, "z", axis=0, tiled=True)
    active = gate_up(core_now, portion, w_gu[0], gu_other, chips)
    everywhere = lax.all_to_all(active, "z", 0, 0, tiled=False)
    outcome = down_project(core_now, everywhere, down, down_other)
    slot_values = lax.all_to_all(outcome, "z", 0, 0, tiled=False)
    beside = [slot_values] + [shifted(slot_values, "x", k) for k in range(1, short)]
    mixed = combine(spread, beside, own_rows)
    out = summed + mixed[0].astype(jnp.float32)
    for k in range(1, long):
        out = out + shifted(mixed[k], "y", k).astype(jnp.float32)
    return out.astype(jnp.bfloat16).reshape(steps, rows_dev, width)


def solution(mesh):
    wide = Mesh(mesh.devices.reshape(8, 2, 4, 4), ("z", "core", "y", "x"))
    group, head = ("z", "core"), ("y", "x")
    both = group + head
    placed = (
        P(None, both, None),
        P(None, both, None, None),
        P(None, both, None),
        P(both, None, None),
        P(both),
        P(head, None, group, None),
        P(head, None),
        P(head, None),
        P(head, None, None),
        P(head, group),
        P(),
        P(None, group, None),
        P(None, group, None),
        P(head, None, None, group),
        P(head, None, group),
    )
    return jax.shard_map(
        per_device,
        mesh=wide,
        in_specs=placed,
        out_specs=P(None, both, None),
        check_vma=False,
    )
```

```python
import functools

import jax
import jax.numpy as jnp
from jax import lax
from jax.experimental import pallas as pl
from jax.experimental.pallas import tpu as pltpu
from jax.sharding import Mesh
from jax.sharding import PartitionSpec as P

LAT = 512
ROPE = 64
VD = 128
CAP = 4
STEPS = 2


def attend(query_rows, key_rows, lengths, recent):
    rows, steps, heads, width = query_rows.shape
    scaling = (VD + ROPE) ** (-0.5)
    flat = query_rows.reshape(rows, steps * heads, width)
    cache_scores = (
        jnp.einsum("nqk,npk->nqp", flat, key_rows, preferred_element_type=jnp.float32) * scaling
    )
    places = lax.broadcasted_iota(jnp.int32, (1, 1, key_rows.shape[1]), 2)
    cache_scores = jnp.where(places < lengths[:, None, None], cache_scores, -jnp.inf)
    fresh_scores = (
        jnp.einsum("nqk,nsk->nqs", flat, recent, preferred_element_type=jnp.float32) * scaling
    )
    step_of = jnp.arange(steps * heads, dtype=jnp.int32)[:, None] // heads
    seen = jnp.arange(steps, dtype=jnp.int32)[None, :] <= step_of
    fresh_scores = jnp.where(seen[None], fresh_scores, -jnp.inf)
    highest = jnp.maximum(jnp.max(cache_scores, axis=2), jnp.max(fresh_scores, axis=2))[:, :, None]
    cache_weights = jnp.exp(cache_scores - highest)
    fresh_weights = jnp.exp(fresh_scores - highest)
    totals = jnp.sum(cache_weights, axis=2, keepdims=True) + jnp.sum(
        fresh_weights, axis=2, keepdims=True
    )
    cache_probs = (cache_weights / totals).astype(jnp.bfloat16)
    fresh_probs = (fresh_weights / totals).astype(jnp.bfloat16)
    context = jnp.einsum(
        "nqp,npl->nql", cache_probs, key_rows[:, :, :LAT], preferred_element_type=jnp.float32
    )
    context = context + jnp.einsum(
        "nqs,nsl->nql", fresh_probs, recent[:, :, :LAT], preferred_element_type=jnp.float32
    )
    return context.astype(jnp.bfloat16).reshape(rows, steps, heads, LAT)


def routing(ids, weights, experts):
    matched = ids[None] == jnp.arange(experts, dtype=jnp.int32)[:, None, None, None]
    present = jnp.any(matched, axis=3)
    row_weight = jnp.sum(jnp.where(matched, weights[None], 0.0), axis=3)
    rows = ids.shape[1]
    before = (
        jnp.arange(rows, dtype=jnp.int32)[:, None] < jnp.arange(rows, dtype=jnp.int32)[None, :]
    )
    slot_index = jnp.einsum(
        "etr,rs->ets",
        present.astype(jnp.bfloat16),
        before.astype(jnp.bfloat16),
        preferred_element_type=jnp.float32,
    ).astype(jnp.int32)
    slots = jnp.arange(CAP, dtype=jnp.int32)[None, None, :, None]
    chosen = (slot_index[:, :, None, :] == slots) & present[:, :, None, :]
    return chosen, row_weight


NT = (((1,), (1,)), ((), ()))


def spread_blocks(block):
    chips = lax.axis_size("z")
    far = chips // 2
    half = block.shape[0] // 2
    own = [None] * chips
    own[0] = [block]
    up = down = block
    for k in range(1, far):
        up, down = shifted(up, "z", 1), shifted(down, "z", -1)
        own[k], own[chips - k] = [up], [down]
    own[far] = [shifted(up[:half], "z", 1), shifted(down[half:], "z", -1)]
    other = [[swap_cores(part) for part in parts] for parts in own]
    return own, other


def project_body(layout, place_ref, x_ref, *refs):
    blocks = refs[: sum(map(sum, layout))]
    *carry, out_ref = refs[len(blocks) :]
    chips = len(layout)
    x = x_ref[...]
    first = place_ref[1] == 0
    at = 0
    for k, counts in enumerate(layout):
        pair = []
        for count in counts:
            parts = [
                lax.dot_general(x, r[...], NT, preferred_element_type=jnp.float32)
                for r in blocks[at : at + count]
            ]
            pair.append(parts[0] if count == 1 else jnp.concatenate(parts, axis=1))
            at += count
        whole = jnp.concatenate(
            [jnp.where(first, pair[0], pair[1]), jnp.where(first, pair[1], pair[0])], axis=1
        )
        width = whole.shape[1]
        chip = lax.rem(place_ref[0] + (chips - k), chips)
        columns = pl.ds(pl.multiple_of(chip * width, 128), width)
        if carry:
            own_ref, hidden_ref = carry
            whole += jnp.dot(
                own_ref[...], hidden_ref[:, columns], preferred_element_type=jnp.float32
            )
        out_ref[:, columns] = whole.astype(jnp.bfloat16)


def project(place, x, own, other, carry=()):
    layout = [(len(a), len(b)) for a, b in zip(own, other)]
    blocks = [part for pair in zip(own, other) for parts in pair for part in parts]
    rows, depth = x.shape
    width = sum(part.shape[0] for part in blocks)
    vmem = pl.BlockSpec(memory_space=pltpu.VMEM)
    return pl.pallas_call(
        functools.partial(project_body, layout),
        in_specs=[pl.BlockSpec(memory_space=pltpu.SMEM)] + [vmem] * (1 + len(blocks) + len(carry)),
        out_specs=vmem,
        out_shape=jax.ShapeDtypeStruct((rows, width), jnp.bfloat16),
        compiler_params=pltpu.CompilerParams(vmem_limit_bytes=24 * 1024 * 1024),
        cost_estimate=pl.CostEstimate(
            flops=2 * rows * depth * width,
            bytes_accessed=2 * depth * width + 2 * rows * width,
            transcendentals=0,
        ),
        name="project_slots" if carry else "project_rows",
    )(place, x, *blocks, *carry)


def after_body(x_ref, other_ref, out_ref):
    del x_ref, other_ref, out_ref


def after(x, other):
    return pl.pallas_call(
        after_body,
        in_specs=[pl.BlockSpec(memory_space=pl.ANY)] * 2,
        out_specs=pl.BlockSpec(memory_space=pl.ANY),
        out_shape=jax.ShapeDtypeStruct(x.shape, x.dtype),
        input_output_aliases={0: 0},
        name="after",
    )(x, other)


def gate_up_body(core_ref, x_ref, own_ref, other_ref, active_ref, gate, up):
    step = pl.program_id(0)

    @pl.when(step == 0)
    def _():
        gate[...] = jnp.zeros_like(gate)
        up[...] = jnp.zeros_like(up)

    x = x_ref[...]
    for part, total in ((0, gate), (1, up)):
        both = jnp.concatenate([own_ref[part], other_ref[part]], axis=1)
        total[...] += jnp.dot(x, both, preferred_element_type=jnp.float32)

    @pl.when(step == pl.num_programs(0) - 1)
    def _():
        g = gate[...]
        active = (g * jax.nn.sigmoid(g) * up[...]).astype(jnp.bfloat16)
        units = active.shape[1] // 2
        first, second = active[:, :units], active[:, units:]

        @pl.when(core_ref[0] == 0)
        def _():
            for k in range(active_ref.shape[0]):
                active_ref[k, :, :units] = first
                active_ref[k, :, units:] = second

        @pl.when(core_ref[0] != 0)
        def _():
            for k in range(active_ref.shape[0]):
                active_ref[k, :, :units] = second
                active_ref[k, :, units:] = first


def gate_up(core, x, own, other, copies):
    rows, depth = x.shape
    units = own.shape[2]
    tile = depth // 4
    return pl.pallas_call(
        gate_up_body,
        grid=(depth // tile,),
        in_specs=[
            pl.BlockSpec(memory_space=pltpu.SMEM),
            pl.BlockSpec((rows, tile), lambda i: (0, i)),
            pl.BlockSpec((2, tile, units), lambda i: (0, i, 0)),
            pl.BlockSpec((2, tile, units), lambda i: (0, i, 0)),
        ],
        out_specs=pl.BlockSpec((copies, rows, 2 * units), lambda i: (0, 0, 0)),
        out_shape=jax.ShapeDtypeStruct((copies, rows, 2 * units), jnp.bfloat16),
        scratch_shapes=[pltpu.VMEM((rows, 2 * units), jnp.float32)] * 2,
        compiler_params=pltpu.CompilerParams(vmem_limit_bytes=24 * 1024 * 1024),
        cost_estimate=pl.CostEstimate(
            flops=8 * rows * depth * units,
            bytes_accessed=8 * depth * units + 2 * rows * depth,
            transcendentals=2 * rows * units,
        ),
        name="gate_up",
    )(core, x, own, other)


def down_body(core_ref, x_ref, own_ref, other_ref, ready_ref, out_ref):
    del ready_ref
    x = jnp.concatenate([x_ref[k] for k in range(x_ref.shape[0])], axis=1)
    half = own_ref.shape[0]
    parts, each = out_ref.shape[0], out_ref.shape[1]
    mine = lax.dot_general(x, own_ref[...], NT, preferred_element_type=jnp.float32)
    others = lax.dot_general(x, other_ref[...], NT, preferred_element_type=jnp.float32)

    def write(first, second):
        both = jnp.concatenate([first, second], axis=1).reshape(parts, each, 2 * half)
        out_ref[...] = both.astype(jnp.bfloat16)

    @pl.when(core_ref[0] == 0)
    def _():
        write(mine, others)

    @pl.when(core_ref[0] != 0)
    def _():
        write(others, mine)


def down_project(core, x, own, other, ready):
    parts, rows, _ = x.shape
    columns = 2 * own.shape[0]
    vmem = pl.BlockSpec(memory_space=pltpu.VMEM)
    return pl.pallas_call(
        down_body,
        in_specs=[
            pl.BlockSpec(memory_space=pltpu.SMEM),
            vmem,
            vmem,
            vmem,
            pl.BlockSpec(memory_space=pl.ANY),
        ],
        out_specs=vmem,
        out_shape=jax.ShapeDtypeStruct((parts, rows // parts, columns), jnp.bfloat16),
        compiler_params=pltpu.CompilerParams(vmem_limit_bytes=24 * 1024 * 1024),
        cost_estimate=pl.CostEstimate(
            flops=2 * rows * own.shape[1] * columns,
            bytes_accessed=2 * own.shape[1] * columns,
            transcendentals=0,
        ),
        name="down_project",
    )(core, x, own, other, ready)


def combine_body(spread_ref, *refs):
    blocks, out_ref = refs[:-1], refs[-1]
    weight = spread_ref[...]
    high = weight.astype(jnp.bfloat16)
    low = (weight - high.astype(jnp.float32)).astype(jnp.bfloat16)
    parts, _, width = blocks[0].shape
    for k in range(parts):
        slots = jnp.concatenate([b[k].astype(jnp.float32) for b in blocks], axis=0)
        slots = slots.astype(jnp.bfloat16)
        mixed = jnp.dot(high, slots, preferred_element_type=jnp.float32) + jnp.dot(
            low, slots, preferred_element_type=jnp.float32
        )
        mixed = mixed.astype(jnp.bfloat16).reshape(*out_ref.shape[:2], width)
        out_ref[:, :, k * width : (k + 1) * width] = mixed


def combine(spread, blocks, each):
    rows = spread.shape[0]
    width = blocks[0].shape[0] * blocks[0].shape[2]
    vmem = pl.BlockSpec(memory_space=pltpu.VMEM)
    return pl.pallas_call(
        combine_body,
        in_specs=[vmem] * (1 + len(blocks)),
        out_specs=vmem,
        out_shape=jax.ShapeDtypeStruct((rows // each, each, width), jnp.bfloat16),
        compiler_params=pltpu.CompilerParams(vmem_limit_bytes=16 * 1024 * 1024),
        cost_estimate=pl.CostEstimate(
            flops=4 * rows * spread.shape[1] * width,
            bytes_accessed=2 * (rows + spread.shape[1]) * width,
            transcendentals=0,
        ),
        name="combine",
    )(spread, *blocks)


def shifted(x, axis, by):
    size = lax.axis_size(axis)
    return lax.ppermute(x, axis, [(i, (i + by) % size) for i in range(size)])


def swap_cores(x):
    return lax.ppermute(x, "core", [(0, 1), (1, 0)])


def per_device(
    hidden_in,
    queries,
    fresh,
    res_cache,
    res_len,
    pre_cache,
    pre_len,
    arrival,
    w_uv,
    w_o,
    norm_gain,
    expert_ids,
    route_weight,
    w_gu,
    w_down,
):
    group, head = ("z", "core"), ("y", "x")
    chips, cores, long, short = (lax.axis_size(a) for a in ("z", "core", "y", "x"))
    groups, columns = chips * cores, long * short
    core, at_y, at_x = (lax.axis_index(a) for a in ("core", "y", "x"))
    group_index = lax.axis_index(group)
    head_index = lax.axis_index(head)
    steps, rows_dev, width = hidden_in.shape
    resident = res_cache.shape[0]
    newcomers = rows_dev - resident
    requests = arrival.shape[1]
    own_rows = steps * rows_dev
    rows_group = columns * own_rows
    heads_dev = w_uv.shape[0]
    slots_dev = steps * CAP

    place = jnp.stack([lax.axis_index("z"), core]).astype(jnp.int32)
    w_own, w_other = spread_blocks(w_o.T)
    gu_other = swap_cores(w_gu[0])
    down = w_down[0].T
    down_other = swap_cores(down)

    places = jnp.arange(requests, dtype=jnp.int32)
    arrival_row = arrival[0]
    claimed = arrival_row[None, :] == places[:, None]
    order = jnp.sum(jnp.where(claimed, places[None, :], 0), axis=1)
    len_sorted = jnp.sum(jnp.where(claimed, pre_len[0][None, :], 0), axis=1)
    new_len = lax.dynamic_slice(len_sorted, (group_index * newcomers,), (newcomers,))
    sorted_cache = jnp.take(pre_cache[0], order, axis=0, mode="clip")
    taken = lax.all_to_all(
        sorted_cache.reshape(groups, newcomers, *sorted_cache.shape[1:]),
        group,
        split_axis=0,
        concat_axis=0,
        tiled=False,
    )
    taken = jnp.swapaxes(taken, 0, 1).reshape(newcomers, -1, sorted_cache.shape[2])

    chosen, row_weight = routing(expert_ids, route_weight, columns)
    by_row = chosen.reshape(columns, steps, CAP, columns, rows_dev)
    same = jnp.arange(steps)[:, None] == jnp.arange(steps)[None, :]
    chooser = by_row[:, :, :, :, None, :] & same[None, :, None, None, :, None]
    chooser = chooser.reshape(columns * slots_dev, rows_group).astype(jnp.bfloat16)
    own_chooser = lax.dynamic_slice(
        chooser, (0, head_index * own_rows), (columns * slots_dev, own_rows)
    )
    near = jnp.where(chosen, row_weight[:, :, None, :], 0.0)
    expert_of = at_y * short + (at_x - jnp.arange(short, dtype=jnp.int32)) % short
    row_of = ((at_y + jnp.arange(long, dtype=jnp.int32)) % long * short + at_x) * rows_dev
    row_of = (row_of[:, None] + jnp.arange(rows_dev, dtype=jnp.int32)[None, :]).reshape(-1)
    pick_expert = expert_of[:, None] == jnp.arange(columns, dtype=jnp.int32)[None, :]
    pick_row = row_of[:, None] == jnp.arange(columns * rows_dev, dtype=jnp.int32)[None, :]
    exact = dict(precision=lax.Precision.HIGHEST, preferred_element_type=jnp.float32)
    near = jnp.einsum("je,etcr->jtcr", pick_expert.astype(jnp.float32), near, **exact)
    near = jnp.einsum("jtcr,qr->jtcq", near, pick_row.astype(jnp.float32), **exact)
    near = near.reshape(short, steps, CAP, long, rows_dev).transpose(3, 4, 0, 1, 2)
    spread = jnp.where(same[None, :, None, None, :, None], near[:, None], 0.0)
    spread = spread.reshape(long * own_rows, short * slots_dev)

    by_row_queries = jnp.swapaxes(queries, 0, 1)
    recent = jnp.swapaxes(fresh, 0, 1)
    context = jnp.concatenate(
        [
            attend(by_row_queries[:resident], res_cache, res_len, recent[:resident]),
            attend(by_row_queries[resident:], taken, new_len, recent[resident:]),
        ],
        axis=0,
    )
    context = context.reshape(rows_dev, steps, columns, heads_dev, LAT).transpose(2, 3, 1, 0, 4)
    by_head = lax.all_to_all(context, head, split_axis=0, concat_axis=0, tiled=False)
    by_head = jnp.swapaxes(by_head, 0, 1).reshape(heads_dev, rows_group, LAT)
    values = jnp.einsum("hrl,hlv->rhv", by_head, w_uv, preferred_element_type=jnp.float32).astype(
        jnp.bfloat16
    )
    values = values.reshape(rows_group, heads_dev * VD)
    values_slots = jnp.dot(chooser, values, preferred_element_type=jnp.float32).astype(jnp.bfloat16)
    hidden_own = hidden_in.reshape(own_rows, width)
    part_slots = project(place, values_slots, w_own, w_other, (own_chooser, hidden_own))
    slot_parts = lax.all_to_all(
        part_slots.reshape(columns, slots_dev, width), head, 0, 0, tiled=False
    )
    part_rows = project(place, values, w_own, w_other)
    slot_rows = jnp.sum(slot_parts.astype(jnp.float32), axis=0)
    normed = (
        slot_rows
        * lax.rsqrt(jnp.mean(slot_rows * slot_rows, axis=1, keepdims=True) + 1e-06)
        * norm_gain
    ).astype(jnp.bfloat16)

    row_parts = lax.all_to_all(
        after(part_rows.reshape(columns, own_rows, width), normed), head, 0, 0, tiled=False
    )
    summed = hidden_own.astype(jnp.float32) + jnp.sum(row_parts.astype(jnp.float32), axis=0)

    core_now = jnp.reshape(core, (1,)).astype(jnp.int32)
    portion = lax.all_gather(normed, "z", axis=0, tiled=True)
    active = gate_up(core_now, portion, w_gu[0], gu_other, chips)
    everywhere = lax.all_to_all(active, "z", 0, 0, tiled=False)
    outcome = down_project(core_now, everywhere, down, down_other, row_parts)
    slot_values = lax.all_to_all(outcome, "z", 0, 0, tiled=False)
    beside = [slot_values] + [shifted(slot_values, "x", k) for k in range(1, short)]
    mixed = combine(spread, beside, own_rows)
    out = summed + mixed[0].astype(jnp.float32)
    for k in range(1, long):
        out = out + shifted(mixed[k], "y", k).astype(jnp.float32)
    return out.astype(jnp.bfloat16).reshape(steps, rows_dev, width)


def solution(mesh):
    wide = Mesh(mesh.devices.reshape(8, 2, 4, 4), ("z", "core", "y", "x"))
    group, head = ("z", "core"), ("y", "x")
    both = group + head
    placed = (
        P(None, both, None),
        P(None, both, None, None),
        P(None, both, None),
        P(both, None, None),
        P(both),
        P(head, None, group, None),
        P(head, None),
        P(head, None),
        P(head, None, None),
        P(head, group),
        P(),
        P(None, group, None),
        P(None, group, None),
        P(head, None, None, group),
        P(head, None, group),
    )
    return jax.shard_map(
        per_device,
        mesh=wide,
        in_specs=placed,
        out_specs=P(None, both, None),
        check_vma=False,
    )
```

```python
import functools

import jax
import jax.numpy as jnp
from jax import lax
from jax.experimental import pallas as pl
from jax.experimental.pallas import tpu as pltpu
from jax.sharding import Mesh
from jax.sharding import PartitionSpec as P

LAT = 512
ROPE = 64
VD = 128
CAP = 4
STEPS = 2


def attend(query_rows, key_rows, lengths, recent):
    rows, steps, heads, width = query_rows.shape
    scaling = (VD + ROPE) ** (-0.5)
    flat = query_rows.reshape(rows, steps * heads, width)
    cache_scores = (
        jnp.einsum("nqk,npk->nqp", flat, key_rows, preferred_element_type=jnp.float32) * scaling
    )
    places = lax.broadcasted_iota(jnp.int32, (1, 1, key_rows.shape[1]), 2)
    cache_scores = jnp.where(places < lengths[:, None, None], cache_scores, -jnp.inf)
    fresh_scores = (
        jnp.einsum("nqk,nsk->nqs", flat, recent, preferred_element_type=jnp.float32) * scaling
    )
    step_of = jnp.arange(steps * heads, dtype=jnp.int32)[:, None] // heads
    seen = jnp.arange(steps, dtype=jnp.int32)[None, :] <= step_of
    fresh_scores = jnp.where(seen[None], fresh_scores, -jnp.inf)
    highest = jnp.maximum(jnp.max(cache_scores, axis=2), jnp.max(fresh_scores, axis=2))[:, :, None]
    cache_weights = jnp.exp(cache_scores - highest)
    fresh_weights = jnp.exp(fresh_scores - highest)
    totals = jnp.sum(cache_weights, axis=2, keepdims=True) + jnp.sum(
        fresh_weights, axis=2, keepdims=True
    )
    cache_probs = (cache_weights / totals).astype(jnp.bfloat16)
    fresh_probs = (fresh_weights / totals).astype(jnp.bfloat16)
    context = jnp.einsum(
        "nqp,npl->nql", cache_probs, key_rows[:, :, :LAT], preferred_element_type=jnp.float32
    )
    context = context + jnp.einsum(
        "nqs,nsl->nql", fresh_probs, recent[:, :, :LAT], preferred_element_type=jnp.float32
    )
    return context.astype(jnp.bfloat16).reshape(rows, steps, heads, LAT)


def routing(ids, weights, experts):
    matched = ids[None] == experts[:, None, None, None]
    present = jnp.any(matched, axis=3)
    row_weight = jnp.sum(jnp.where(matched, weights[None], 0.0), axis=3)
    rows = ids.shape[1]
    before = (
        jnp.arange(rows, dtype=jnp.int32)[:, None] < jnp.arange(rows, dtype=jnp.int32)[None, :]
    )
    slot_index = jnp.einsum(
        "etr,rs->ets",
        present.astype(jnp.bfloat16),
        before.astype(jnp.bfloat16),
        preferred_element_type=jnp.float32,
    ).astype(jnp.int32)
    slots = jnp.arange(CAP, dtype=jnp.int32)[None, None, :, None]
    chosen = (slot_index[:, :, None, :] == slots) & present[:, :, None, :]
    return chosen, row_weight


NT = (((1,), (1,)), ((), ()))


def part_body(start, block_ref, ready_ref, out_ref, sem):
    del ready_ref
    copy = pltpu.make_async_copy(block_ref.at[pl.ds(start, out_ref.shape[0])], out_ref, sem)
    copy.start()
    copy.wait()


def part_after(block, start, size, ready):
    anywhere = pl.BlockSpec(memory_space=pltpu.HBM)
    return pl.pallas_call(
        functools.partial(part_body, start),
        in_specs=[anywhere, anywhere],
        out_specs=anywhere,
        out_shape=jax.ShapeDtypeStruct((size, block.shape[1]), block.dtype),
        scratch_shapes=[pltpu.SemaphoreType.DMA(())],
        name="part_after",
    )(block, ready)


def spread_blocks(block):
    up = down = block
    steps = []
    for _ in range(1, lax.axis_size("z") // 2):
        up, down = shifted(up, "z", 1), shifted(down, "z", -1)
        steps.append((up, down))
    return steps


def all_blocks(block, steps, ready):
    half = block.shape[0] // 2
    (up, down), far = steps[-1], lax.axis_size("z") // 2
    last = [
        shifted(part_after(up, 0, half, ready), "z", 1),
        shifted(part_after(down, half, half, ready), "z", -1),
    ]
    own = [[block]] + [[u] for u, _ in steps] + [last] + [[d] for _, d in steps[::-1]]
    assert len(own) == 2 * far
    return own, [[swap_cores(part) for part in parts] for parts in own]


def project_body(layout, place_ref, by_ref, uv_ref, select_ref, own_ref, hidden_ref, *refs):
    total = sum(map(sum, layout))
    blocks, outs = refs[:total], refs[total:-5]
    held, slots_ref, rows_ref, sems, out_sems = refs[-5:]
    chips = len(layout)
    copies, at, start = [], 0, 0
    for counts in layout:
        for count in counts:
            for r in blocks[at : at + count]:
                size = r.shape[0]
                copies.append(pltpu.make_async_copy(r, held.at[pl.ds(start, size)], sems.at[at]))
                copies[-1].start()
                at, start = at + 1, start + size
    values = []
    for k in range(uv_ref.shape[0]):
        context = by_ref[:, k].astype(jnp.float32).reshape(-1, by_ref.shape[3])
        values.append(
            jnp.dot(context.astype(jnp.bfloat16), uv_ref[k], preferred_element_type=jnp.float32)
        )
    values = jnp.concatenate(values, axis=1).astype(jnp.bfloat16)
    x = jnp.dot(select_ref[...], values, preferred_element_type=jnp.float32).astype(jnp.bfloat16)
    half = slots_ref.shape[0]
    each = rows_ref.shape[1]
    first = place_ref[1] == 0
    at, start = 0, 0
    width = held.shape[0] // chips
    core_width = width // 2
    leaving = []
    for k, counts in enumerate(layout):
        for _ in range(sum(counts)):
            copies[at].wait()
            at += 1
        pair = [
            lax.dot_general(
                x,
                held[start + c * core_width : start + (c + 1) * core_width],
                NT,
                preferred_element_type=jnp.float32,
            )
            for c in range(2)
        ]
        start += width
        whole = jnp.concatenate(
            [jnp.where(first, pair[0], pair[1]), jnp.where(first, pair[1], pair[0])], axis=1
        )
        chip = lax.rem(place_ref[0] + (chips - k), chips)
        columns = pl.ds(pl.multiple_of(chip * width, 128), width)
        carried = jnp.dot(own_ref[...], hidden_ref[:, columns], preferred_element_type=jnp.float32)
        slots_ref[:, columns] = (whole[:half] + carried).astype(jnp.bfloat16)
        for j in range(rows_ref.shape[0]):
            row = half + j * each
            rows_ref[j, :, columns] = whole[row : row + each].astype(jnp.bfloat16)
        for j, out_ref in enumerate(outs):
            source = slots_ref if j == 0 else rows_ref.at[j - 1]
            leaving.append(
                pltpu.make_async_copy(
                    source.at[:, columns], out_ref.at[:, columns], out_sems.at[j, k]
                )
            )
            leaving[-1].start()
    for copy in leaving:
        copy.wait()


def project(place, by_head, w_uv, select, own, other, chooser, hidden, outer, inner):
    layout = [(len(a), len(b)) for a, b in zip(own, other)]
    blocks = [part for pair in zip(own, other) for parts in pair for part in parts]
    rows, depth = select.shape[0], blocks[0].shape[1]
    half = rows // 2
    width = sum(part.shape[0] for part in blocks)
    each = half // inner
    vmem = pl.BlockSpec(memory_space=pltpu.VMEM)
    anywhere = pl.BlockSpec(memory_space=pltpu.HBM)
    return pl.pallas_call(
        functools.partial(project_body, layout),
        in_specs=[pl.BlockSpec(memory_space=pltpu.SMEM)] + [vmem] * 5 + [anywhere] * len(blocks),
        out_specs=[anywhere] * (1 + inner),
        out_shape=[jax.ShapeDtypeStruct((half, width), jnp.bfloat16)]
        + [jax.ShapeDtypeStruct((each, width), jnp.bfloat16)] * inner,
        scratch_shapes=[
            pltpu.VMEM((width, depth), jnp.bfloat16),
            pltpu.VMEM((half, width), jnp.bfloat16),
            pltpu.VMEM((inner, each, width), jnp.bfloat16),
            pltpu.SemaphoreType.DMA((len(blocks),)),
            pltpu.SemaphoreType.DMA((1 + inner, len(layout))),
        ],
        compiler_params=pltpu.CompilerParams(vmem_limit_bytes=58 * 1024 * 1024),
        cost_estimate=pl.CostEstimate(
            flops=2 * rows * depth * width,
            bytes_accessed=2 * depth * width + 2 * rows * width,
            transcendentals=0,
        ),
        name="project",
    )(place, by_head, w_uv, select, chooser, hidden, *blocks)


def after_body(*refs):
    del refs


def after(x, *others):
    return pl.pallas_call(
        after_body,
        in_specs=[pl.BlockSpec(memory_space=pltpu.HBM)] * (1 + len(others)),
        out_specs=pl.BlockSpec(memory_space=pltpu.HBM),
        out_shape=jax.ShapeDtypeStruct(x.shape, x.dtype),
        input_output_aliases={0: 0},
        name="after",
    )(x, *others)


def norm_body(parts_ref, gain_ref, *refs):
    total, out_ref = refs[-1], refs[(len(refs) - 2) // 2]
    parts, _, width = parts_ref.shape
    tile = width // 8
    squares = 0.0
    for k in range(8):
        at = slice(k * tile, (k + 1) * tile)
        here = parts_ref[0, :, at].astype(jnp.float32)
        for j in range(1, parts):
            here += parts_ref[j, :, at].astype(jnp.float32)
        total[:, at] = here
        squares += jnp.sum(here * here, axis=1, keepdims=True)
    scale = lax.rsqrt(squares * (1.0 / width) + 1e-06)
    for k in range(8):
        at = slice(k * tile, (k + 1) * tile)
        out_ref[:, at] = (total[:, at] * scale * gain_ref[:, at]).astype(jnp.bfloat16)


def norm(parts, gain, held):
    _, rows, width = parts.shape
    vmem = pl.BlockSpec(memory_space=pltpu.VMEM)
    anywhere = pl.BlockSpec(memory_space=pltpu.HBM)
    return pl.pallas_call(
        norm_body,
        in_specs=[vmem, vmem] + [anywhere] * len(held),
        out_specs=[vmem] + [anywhere] * len(held),
        out_shape=[jax.ShapeDtypeStruct((rows, width), jnp.bfloat16)]
        + [jax.ShapeDtypeStruct(h.shape, h.dtype) for h in held],
        scratch_shapes=[pltpu.VMEM((rows, width), jnp.float32)],
        input_output_aliases={2 + k: 1 + k for k in range(len(held))},
        compiler_params=pltpu.CompilerParams(vmem_limit_bytes=16 * 1024 * 1024),
        cost_estimate=pl.CostEstimate(
            flops=2 * parts.size, bytes_accessed=2 * parts.size, transcendentals=0
        ),
        name="norm",
    )(parts, gain, *held)


def gate_up_body(core_ref, x_ref, own_ref, other_ref, active_ref, gate, up):
    step = pl.program_id(0)

    @pl.when(step == 0)
    def _():
        gate[...] = jnp.zeros_like(gate)
        up[...] = jnp.zeros_like(up)

    x = x_ref[...]
    for part, total in ((0, gate), (1, up)):
        both = jnp.concatenate([own_ref[part], other_ref[part]], axis=1)
        total[...] += jnp.dot(x, both, preferred_element_type=jnp.float32)

    @pl.when(step == pl.num_programs(0) - 1)
    def _():
        g = gate[...]
        active = (g * jax.nn.sigmoid(g) * up[...]).astype(jnp.bfloat16)
        units = active.shape[1] // 2
        first, second = active[:, :units], active[:, units:]

        @pl.when(core_ref[0] == 0)
        def _():
            for k in range(active_ref.shape[0]):
                active_ref[k, :, :units] = first
                active_ref[k, :, units:] = second

        @pl.when(core_ref[0] != 0)
        def _():
            for k in range(active_ref.shape[0]):
                active_ref[k, :, :units] = second
                active_ref[k, :, units:] = first


def gate_up(core, x, own, other, copies):
    rows, depth = x.shape
    units = own.shape[2]
    tile = depth // 4
    return pl.pallas_call(
        gate_up_body,
        grid=(depth // tile,),
        in_specs=[
            pl.BlockSpec(memory_space=pltpu.SMEM),
            pl.BlockSpec((rows, tile), lambda i: (0, i)),
            pl.BlockSpec((2, tile, units), lambda i: (0, i, 0)),
            pl.BlockSpec((2, tile, units), lambda i: (0, i, 0)),
        ],
        out_specs=pl.BlockSpec((copies, rows, 2 * units), lambda i: (0, 0, 0)),
        out_shape=jax.ShapeDtypeStruct((copies, rows, 2 * units), jnp.bfloat16),
        scratch_shapes=[pltpu.VMEM((rows, 2 * units), jnp.float32)] * 2,
        compiler_params=pltpu.CompilerParams(vmem_limit_bytes=24 * 1024 * 1024),
        cost_estimate=pl.CostEstimate(
            flops=8 * rows * depth * units,
            bytes_accessed=8 * depth * units + 2 * rows * depth,
            transcendentals=2 * rows * units,
        ),
        name="gate_up",
    )(core, x, own, other)


def down_body(core_ref, x_ref, own_ref, other_ref, *refs):
    out_ref = refs[-1]
    x = jnp.concatenate([x_ref[k] for k in range(x_ref.shape[0])], axis=1)
    half = own_ref.shape[0]
    parts, each = out_ref.shape[0], out_ref.shape[1]
    mine = lax.dot_general(x, own_ref[...], NT, preferred_element_type=jnp.float32)
    others = lax.dot_general(x, other_ref[...], NT, preferred_element_type=jnp.float32)

    def write(first, second):
        both = jnp.concatenate([first, second], axis=1).reshape(parts, each, 2 * half)
        out_ref[...] = both.astype(jnp.bfloat16)

    @pl.when(core_ref[0] == 0)
    def _():
        write(mine, others)

    @pl.when(core_ref[0] != 0)
    def _():
        write(others, mine)


def down_project(core, x, own, other, *ready):
    parts, rows, _ = x.shape
    columns = 2 * own.shape[0]
    vmem = pl.BlockSpec(memory_space=pltpu.VMEM)
    return pl.pallas_call(
        down_body,
        in_specs=[
            pl.BlockSpec(memory_space=pltpu.SMEM),
            vmem,
            vmem,
            vmem,
            *[pl.BlockSpec(memory_space=pltpu.HBM)] * len(ready),
        ],
        out_specs=vmem,
        out_shape=jax.ShapeDtypeStruct((parts, rows // parts, columns), jnp.bfloat16),
        compiler_params=pltpu.CompilerParams(vmem_limit_bytes=24 * 1024 * 1024),
        cost_estimate=pl.CostEstimate(
            flops=2 * rows * own.shape[1] * columns,
            bytes_accessed=2 * own.shape[1] * columns,
            transcendentals=0,
        ),
        name="down_project",
    )(core, x, own, other, *ready)


def combine_body(count, spread_ref, hidden_ref, *refs):
    blocks, sums, (here_ref, *away) = refs[:count], refs[count : 2 * count], refs[2 * count :]
    weight = spread_ref[...]
    high = weight.astype(jnp.bfloat16)
    low = (weight - high.astype(jnp.float32)).astype(jnp.bfloat16)
    parts, _, width = blocks[0].shape
    each = here_ref.shape[0]
    for k in range(parts):
        slots = jnp.concatenate([b[k].astype(jnp.float32) for b in blocks], axis=0)
        slots = slots.astype(jnp.bfloat16)
        mixed = jnp.dot(high, slots, preferred_element_type=jnp.float32) + jnp.dot(
            low, slots, preferred_element_type=jnp.float32
        )
        at = slice(k * width, (k + 1) * width)
        for r in sums:
            mixed += r[:, at].astype(jnp.float32)
        for y in range(1 + len(away)):
            row = mixed[y * each : (y + 1) * each]
            if y == 0:
                here_ref[:, at] = row + hidden_ref[:, at].astype(jnp.float32)
            else:
                away[y - 1][:, at] = row.astype(jnp.bfloat16)


def combine(spread, hidden, blocks, sums):
    each, width = hidden.shape
    outer = spread.shape[0] // each
    vmem = pl.BlockSpec(memory_space=pltpu.VMEM)
    away = jax.ShapeDtypeStruct((each, width), jnp.bfloat16)
    return pl.pallas_call(
        functools.partial(combine_body, len(blocks)),
        in_specs=[vmem] * (2 + len(blocks) + len(sums)),
        out_specs=[vmem] * outer,
        out_shape=[jax.ShapeDtypeStruct((each, width), jnp.float32)] + [away] * (outer - 1),
        compiler_params=pltpu.CompilerParams(vmem_limit_bytes=16 * 1024 * 1024),
        cost_estimate=pl.CostEstimate(
            flops=4 * spread.shape[0] * spread.shape[1] * width,
            bytes_accessed=10 * spread.shape[0] * width,
            transcendentals=0,
        ),
        name="combine",
    )(spread, hidden, *blocks, *sums)


def shifted(x, axis, by):
    size = lax.axis_size(axis)
    return lax.ppermute(x, axis, [(i, (i + by) % size) for i in range(size)])


def swap_cores(x):
    return lax.ppermute(x, "core", [(0, 1), (1, 0)])


def per_device(
    hidden_in,
    queries,
    fresh,
    res_cache,
    res_len,
    pre_cache,
    pre_len,
    arrival,
    w_uv,
    w_o,
    norm_gain,
    expert_ids,
    route_weight,
    w_gu,
    w_down,
):
    group, head = ("z", "core"), ("y", "x")
    chips, cores, long, short = (lax.axis_size(a) for a in ("z", "core", "y", "x"))
    groups, columns = chips * cores, long * short
    core, at_y, at_x = (lax.axis_index(a) for a in ("core", "y", "x"))
    group_index = lax.axis_index(group)
    head_index = lax.axis_index(head)
    steps, rows_dev, width = hidden_in.shape
    resident = res_cache.shape[0]
    newcomers = rows_dev - resident
    requests = arrival.shape[1]
    own_rows = steps * rows_dev
    rows_group = columns * own_rows
    heads_dev = w_uv.shape[0]
    slots_dev = steps * CAP

    place = jnp.stack([lax.axis_index("z"), core]).astype(jnp.int32)
    ring = spread_blocks(w_o.T)
    came = [[part[:8, :128] for part in parts] for parts in ring]
    experts = after(jnp.arange(columns, dtype=jnp.int32), *came[0])
    res_len = after(res_len, *came[0])
    gu_other = swap_cores(w_gu[0])
    down = w_down[0].T
    down_other = swap_cores(down)

    places = jnp.arange(requests, dtype=jnp.int32)
    arrival_row = arrival[0]
    claimed = arrival_row[None, :] == places[:, None]
    order = jnp.sum(jnp.where(claimed, places[None, :], 0), axis=1)
    len_sorted = jnp.sum(jnp.where(claimed, pre_len[0][None, :], 0), axis=1)
    new_len = lax.dynamic_slice(len_sorted, (group_index * newcomers,), (newcomers,))
    new_len = after(new_len, *came[1])
    sorted_cache = jnp.take(pre_cache[0], order, axis=0, mode="clip")
    taken = lax.all_to_all(
        sorted_cache.reshape(groups, newcomers, *sorted_cache.shape[1:]),
        group,
        split_axis=0,
        concat_axis=0,
        tiled=False,
    )
    taken = jnp.swapaxes(taken, 0, 1).reshape(newcomers, -1, sorted_cache.shape[2])

    chosen, row_weight = routing(expert_ids, route_weight, experts)
    by_row = chosen.reshape(columns, steps, CAP, columns, rows_dev)
    same = jnp.arange(steps)[:, None] == jnp.arange(steps)[None, :]
    chooser = by_row[:, :, :, :, None, :] & same[None, :, None, None, :, None]
    chooser = chooser.reshape(columns * slots_dev, rows_group).astype(jnp.bfloat16)
    own_chooser = lax.dynamic_slice(
        chooser, (0, head_index * own_rows), (columns * slots_dev, own_rows)
    )
    near = jnp.where(chosen, row_weight[:, :, None, :], 0.0)
    expert_of = at_y * short + (at_x - jnp.arange(short, dtype=jnp.int32)) % short
    row_of = ((at_y + jnp.arange(long, dtype=jnp.int32)) % long * short + at_x) * rows_dev
    row_of = (row_of[:, None] + jnp.arange(rows_dev, dtype=jnp.int32)[None, :]).reshape(-1)
    pick_expert = expert_of[:, None] == jnp.arange(columns, dtype=jnp.int32)[None, :]
    pick_row = row_of[:, None] == jnp.arange(columns * rows_dev, dtype=jnp.int32)[None, :]
    exact = dict(precision=lax.Precision.HIGHEST, preferred_element_type=jnp.float32)
    near = jnp.einsum("je,etcr->jtcr", pick_expert.astype(jnp.float32), near, **exact)
    near = jnp.einsum("jtcr,qr->jtcq", near, pick_row.astype(jnp.float32), **exact)
    near = near.reshape(short, steps, CAP, long, rows_dev).transpose(3, 4, 0, 1, 2)
    spread = jnp.where(same[None, :, None, None, :, None], near[:, None], 0.0)
    spread = spread.reshape(long * own_rows, short * slots_dev)

    by_row_queries = jnp.swapaxes(queries, 0, 1)
    recent = jnp.swapaxes(fresh, 0, 1)
    context = jnp.concatenate(
        [
            attend(by_row_queries[:resident], res_cache, res_len, recent[:resident]),
            attend(by_row_queries[resident:], taken, new_len, recent[resident:]),
        ],
        axis=0,
    )
    context = context.reshape(rows_dev, steps, columns, heads_dev, LAT).transpose(2, 3, 1, 0, 4)
    context = context.reshape(columns, heads_dev, own_rows, LAT)
    w_own, w_other = all_blocks(w_o.T, ring, context[0, 0, :, :128])
    by_head = lax.all_to_all(context, head, split_axis=0, concat_axis=0, tiled=False)
    hidden_own = hidden_in.reshape(own_rows, width)
    from_x = (at_x + jnp.arange(short, dtype=jnp.int32)) % short
    from_y = (at_y + jnp.arange(long, dtype=jnp.int32)) % long
    row_from = (from_y[None, :, None] * short + from_x[:, None, None]) * own_rows
    row_from = (row_from + jnp.arange(own_rows, dtype=jnp.int32)).reshape(-1)
    turned = row_from[:, None] == jnp.arange(rows_group, dtype=jnp.int32)[None, :]
    select = jnp.concatenate([chooser, turned.astype(jnp.bfloat16)], axis=0)
    part_slots, row_here, *row_away = project(
        place, by_head, w_uv, select, w_own, w_other, own_chooser, hidden_own, long, short
    )
    slot_parts = lax.all_to_all(
        part_slots.reshape(columns, slots_dev, width), head, 0, 0, tiled=False
    )
    normed, *row_away = norm(slot_parts, norm_gain[None], row_away)
    row_parts = [row_here] + [shifted(r, "x", k + 1) for k, r in enumerate(row_away)]

    core_now = jnp.reshape(core, (1,)).astype(jnp.int32)
    portion = lax.all_gather(normed, "z", axis=0, tiled=True)
    active = gate_up(core_now, portion, w_gu[0], gu_other, chips)
    everywhere = lax.all_to_all(active, "z", 0, 0, tiled=False)
    outcome = down_project(core_now, everywhere, down, down_other, *row_parts[1:])
    slot_values = lax.all_to_all(outcome, "z", 0, 0, tiled=False)
    beside = [slot_values] + [shifted(slot_values, "x", k) for k in range(1, short)]
    out, *mixed = combine(spread, hidden_own, beside, row_parts)
    for k, part in enumerate(mixed):
        out = out + shifted(part, "y", k + 1).astype(jnp.float32)
    return out.astype(jnp.bfloat16).reshape(steps, rows_dev, width)


def solution(mesh):
    wide = Mesh(mesh.devices.reshape(8, 2, 4, 4), ("z", "core", "y", "x"))
    group, head = ("z", "core"), ("y", "x")
    both = group + head
    placed = (
        P(None, both, None),
        P(None, both, None, None),
        P(None, both, None),
        P(both, None, None),
        P(both),
        P(head, None, group, None),
        P(head, None),
        P(head, None),
        P(head, None, None),
        P(head, group),
        P(),
        P(None, group, None),
        P(None, group, None),
        P(head, None, None, group),
        P(head, None, group),
    )
    return jax.shard_map(
        per_device,
        mesh=wide,
        in_specs=placed,
        out_specs=P(None, both, None),
        check_vma=False,
    )
```

```python
import functools

import jax
import jax.numpy as jnp
from jax import lax
from jax.experimental import pallas as pl
from jax.experimental.pallas import tpu as pltpu
from jax.sharding import Mesh
from jax.sharding import PartitionSpec as P

LAT = 512
ROPE = 64
VD = 128
CAP = 4
STEPS = 2


NT = (((1,), (1,)), ((), ()))


def context_of(query, scores, values, fresh, length):
    scaling = (VD + ROPE) ** (-0.5)
    cached = scores(query) * scaling
    places = lax.broadcasted_iota(jnp.int32, cached.shape, 1)
    cached = jnp.where(places < length, cached, -jnp.inf)
    recent = lax.dot_general(query, fresh, NT, preferred_element_type=jnp.float32) * scaling
    step = lax.broadcasted_iota(jnp.int32, recent.shape, 0) // (query.shape[0] // STEPS)
    recent = jnp.where(lax.broadcasted_iota(jnp.int32, recent.shape, 1) <= step, recent, -jnp.inf)
    highest = jnp.maximum(
        jnp.max(cached, axis=1, keepdims=True), jnp.max(recent, axis=1, keepdims=True)
    )
    cached, recent = jnp.exp(cached - highest), jnp.exp(recent - highest)
    totals = jnp.sum(cached, axis=1, keepdims=True) + jnp.sum(recent, axis=1, keepdims=True)
    cached, recent = (cached / totals).astype(jnp.bfloat16), (recent / totals).astype(jnp.bfloat16)
    mixed = values(cached) + jnp.dot(
        recent, fresh[:, :LAT], preferred_element_type=jnp.float32
    )
    return mixed.astype(jnp.bfloat16)


def attend_resident_body(len_ref, q_ref, keys_ref, fresh_ref, out_ref):
    keys = keys_ref[0]
    query = jnp.concatenate([q_ref[t, 0] for t in range(STEPS)], axis=0)
    out_ref[0] = context_of(
        query,
        lambda q: jnp.dot(q, keys, preferred_element_type=jnp.float32),
        lambda p: lax.dot_general(p, keys[:LAT], NT, preferred_element_type=jnp.float32),
        fresh_ref[0],
        len_ref[pl.program_id(0)],
    )


def attend_resident(lengths, queries, keys, fresh):
    rows, width, places = keys.shape
    steps, _, heads, _ = queries.shape
    return pl.pallas_call(
        attend_resident_body,
        grid=(rows,),
        in_specs=[
            pl.BlockSpec(memory_space=pltpu.SMEM),
            pl.BlockSpec((steps, 1, heads, width), lambda i: (0, i, 0, 0)),
            pl.BlockSpec((1, width, places), lambda i: (i, 0, 0)),
            pl.BlockSpec((1, *fresh.shape[1:]), lambda i: (i, 0, 0)),
        ],
        out_specs=pl.BlockSpec((1, steps * heads, LAT), lambda i: (i, 0, 0)),
        out_shape=jax.ShapeDtypeStruct((rows, steps * heads, LAT), jnp.bfloat16),
        compiler_params=pltpu.CompilerParams(vmem_limit_bytes=24 * 1024 * 1024),
        cost_estimate=pl.CostEstimate(
            flops=4 * keys.size * steps * heads, bytes_accessed=20000000, transcendentals=0
        ),
        name="attend_resident",
    )(lengths, queries, keys, fresh)


def attend_new_body(len_ref, q_ref, taken_ref, fresh_ref, done_ref, *refs):
    out_ref = refs[-1]
    resident, queries, _ = done_ref.shape
    fresh_rows = q_ref.shape[1]
    contexts = [done_ref[n] for n in range(resident)]
    for n in range(fresh_rows):
        keys = taken_ref[:, n].astype(jnp.float32)
        keys = keys.reshape(-1, keys.shape[2]).astype(jnp.bfloat16)
        contexts.append(
            context_of(
                jnp.concatenate([q_ref[t, n] for t in range(STEPS)], axis=0),
                lambda q: lax.dot_general(q, keys, NT, preferred_element_type=jnp.float32),
                lambda p: jnp.dot(p, keys[:, :LAT], preferred_element_type=jnp.float32),
                fresh_ref[n],
                len_ref[n],
            )
        )
    rows = resident + fresh_rows
    context = jnp.concatenate(contexts, axis=0)
    size = context.shape[0]
    heads = queries // STEPS
    to = lax.broadcasted_iota(jnp.int32, (size, size), 0)
    source = to % rows * queries + to // rows % STEPS * heads + to // (rows * STEPS)
    turn = (source == lax.broadcasted_iota(jnp.int32, (size, size), 1)).astype(jnp.float32)
    turned = jnp.dot(turn.astype(jnp.bfloat16), context, preferred_element_type=jnp.float32)
    out_ref[...] = turned.reshape(out_ref.shape).astype(jnp.bfloat16)


def attend_new(lengths, queries, taken, fresh, done, columns, ready):
    _, rows, _, width = taken.shape
    steps, whole, heads, _ = queries.shape
    out = (columns, heads // columns, steps * whole, LAT)
    last = whole // rows - 1
    return pl.pallas_call(
        attend_new_body,
        grid=(1,),
        in_specs=[
            pl.BlockSpec(memory_space=pltpu.SMEM),
            pl.BlockSpec((steps, rows, heads, width), lambda i: (0, last, 0, 0)),
            pl.BlockSpec(taken.shape, lambda i: (0, 0, 0, 0)),
            pl.BlockSpec((rows, *fresh.shape[1:]), lambda i: (last, 0, 0)),
            pl.BlockSpec(done.shape, lambda i: (0, 0, 0)),
        ]
        + [pl.BlockSpec(memory_space=pltpu.HBM)] * len(ready),
        out_specs=pl.BlockSpec(out, lambda i: (0, 0, 0, 0)),
        out_shape=jax.ShapeDtypeStruct(out, jnp.bfloat16),
        compiler_params=pltpu.CompilerParams(vmem_limit_bytes=24 * 1024 * 1024),
        cost_estimate=pl.CostEstimate(
            flops=4 * taken.size * steps * heads, bytes_accessed=20000000, transcendentals=0
        ),
        name="attend_new",
    )(lengths, queries, taken, fresh, done, *ready)


def picked(one_hot, x, dims=(((1,), (0,)), ((), ()))):
    one_hot = one_hot.astype(jnp.float32).astype(jnp.bfloat16)
    total = None
    for _ in range(3):
        part = x.astype(jnp.bfloat16)
        x = x - part.astype(jnp.float32)
        term = lax.dot_general(one_hot, part, dims, preferred_element_type=jnp.float32)
        total = term if total is None else total + term
    return total


def routing_body(sizes, place_ref, ids_ref, weights_ref, *refs):
    long, short, rows_dev = sizes
    select_ref, own_ref, spread_ref, present_ref, weight_ref = refs[-5:]
    steps, _, rows = ids_ref.shape
    columns = long * short
    own_rows, slots = steps * rows_dev, steps * CAP
    at_y, at_x = place_ref[2], place_ref[3]

    def iota(shape, axis):
        return lax.broadcasted_iota(jnp.int32, shape, axis)

    for t in range(steps):
        ids, weights = ids_ref[t], weights_ref[t]
        for e in range(columns):
            at = slice(e * steps + t, e * steps + t + 1)
            matched = ids == e
            present_ref[at] = jnp.max(matched.astype(jnp.float32), axis=0, keepdims=True)
            weight_ref[at] = jnp.sum(jnp.where(matched, weights, 0.0), axis=0, keepdims=True)
    present = present_ref[...]
    before = iota((rows, rows), 0) < iota((rows, rows), 1)
    place = jnp.dot(
        present.astype(jnp.bfloat16),
        before.astype(jnp.float32).astype(jnp.bfloat16),
        preferred_element_type=jnp.float32,
    )
    count = columns * slots
    widen = iota((count, columns * steps), 0) // CAP == iota((count, columns * steps), 1)
    slot = (iota((count, rows), 0) % CAP).astype(jnp.float32)
    chosen = (picked(widen, place) == slot) & (picked(widen, present) > 0.5)
    weighted = jnp.where(chosen, picked(widen, weight_ref[...]), 0.0)
    total = columns * own_rows
    to = iota((rows, total), 1)
    spot = to // own_rows * rows_dev + to % rows_dev == iota((rows, total), 0)
    same = (
        iota((count, total), 0) // CAP % steps == iota((count, total), 1) // rows_dev % steps
    )
    spot = spot.astype(jnp.float32).astype(jnp.bfloat16)
    chooser = jnp.dot(
        chosen.astype(jnp.float32).astype(jnp.bfloat16), spot, preferred_element_type=jnp.float32
    )
    chooser = jnp.where(same, chooser, 0.0).astype(jnp.bfloat16)
    select_ref[:count] = chooser
    to = iota((total, total), 0)
    from_x = (at_x + to // (long * own_rows)) % short
    from_y = (at_y + to // own_rows % long) % long
    source = (from_y * short + from_x) * own_rows + to % own_rows
    turned = source == iota((total, total), 1)
    select_ref[count:] = turned.astype(jnp.float32).astype(jnp.bfloat16)
    head = at_y * short + at_x
    mine = iota((total, own_rows), 0) == head * own_rows + iota((total, own_rows), 1)
    own_ref[...] = jnp.dot(
        chooser, mine.astype(jnp.float32).astype(jnp.bfloat16), preferred_element_type=jnp.float32
    ).astype(jnp.bfloat16)
    to = iota((short * slots, count), 0)
    expert = at_y * short + (at_x + short - to // slots) % short
    near = picked(expert * slots + to % slots == iota((short * slots, count), 1), weighted)
    to = iota((long * own_rows, rows), 0)
    row = ((at_y + to // own_rows) % long * short + at_x) * rows_dev + to % rows_dev
    near = picked(row == iota((long * own_rows, rows), 1), near, NT)
    shape = (long * own_rows, short * slots)
    same = iota(shape, 0) // rows_dev % steps == iota(shape, 1) // CAP % steps
    spread_ref[...] = jnp.where(same, near, 0.0)


def routing(place, ids, weights, long, short, rows_dev, ready):
    steps, _, rows = ids.shape
    count, total = long * short * steps * CAP, rows * steps
    vmem = pl.BlockSpec(memory_space=pltpu.VMEM)
    return pl.pallas_call(
        functools.partial(routing_body, (long, short, rows_dev)),
        in_specs=[
            pl.BlockSpec(memory_space=pltpu.SMEM),
            vmem,
            vmem,
            *[pl.BlockSpec(memory_space=pltpu.HBM)] * len(ready),
        ],
        out_specs=[vmem] * 3,
        out_shape=[
            jax.ShapeDtypeStruct((count + total, total), jnp.bfloat16),
            jax.ShapeDtypeStruct((count, steps * rows_dev), jnp.bfloat16),
            jax.ShapeDtypeStruct((long * steps * rows_dev, short * steps * CAP), jnp.float32),
        ],
        scratch_shapes=[pltpu.VMEM((long * short * steps, rows), jnp.float32)] * 2,
        compiler_params=pltpu.CompilerParams(vmem_limit_bytes=24 * 1024 * 1024),
        cost_estimate=pl.CostEstimate(flops=0, bytes_accessed=10000000, transcendentals=0),
        name="routing",
    )(place, ids, weights, *ready)


def after_body(up_ref, down_ref, ready_ref, out_up_ref, out_down_ref, pair_ref):
    del ready_ref
    for k, (ref, out_ref) in enumerate([(up_ref, out_up_ref), (down_ref, out_down_ref)]):
        block = ref[...]
        out_ref[...] = block
        pair_ref[k] = block


def after(up, down, ready, space):
    vmem = pl.BlockSpec(memory_space=pltpu.VMEM)
    one = jax.ShapeDtypeStruct(up.shape, up.dtype)
    return pl.pallas_call(
        after_body,
        in_specs=[vmem, vmem, pl.BlockSpec(memory_space=space)],
        out_specs=[vmem] * 3,
        out_shape=[one, one, jax.ShapeDtypeStruct((2, *up.shape), up.dtype)],
        compiler_params=pltpu.CompilerParams(vmem_limit_bytes=8 * 1024 * 1024),
        name="after",
    )(up, down, ready)


def halves_body(up_ref, down_ref, ready_ref, first_ref, second_ref):
    del ready_ref
    half = first_ref.shape[0]
    first_ref[...] = up_ref[:half]
    second_ref[...] = down_ref[half:]


def halves(up, down, ready):
    vmem = pl.BlockSpec(memory_space=pltpu.VMEM)
    half = jax.ShapeDtypeStruct((up.shape[0] // 2, up.shape[1]), up.dtype)
    return pl.pallas_call(
        halves_body,
        in_specs=[vmem] * 3,
        out_specs=[vmem] * 2,
        out_shape=[half, half],
        compiler_params=pltpu.CompilerParams(vmem_limit_bytes=8 * 1024 * 1024),
        name="halves",
    )(up, down, ready)


def project_body(layout, place_ref, by_ref, uv_ref, select_ref, own_ref, hidden_ref, *refs):
    total = 1 + max(i for pair in layout for parts in pair for i, _ in parts)
    blocks, outs = refs[:total], refs[total:-5]
    held, slots_ref, rows_ref, sems, out_sems = refs[-5:]
    chips = len(layout)
    copies, start = [], 0
    for pair in layout:
        for i, j in pair[0] + pair[1]:
            r = blocks[i] if j is None else blocks[i].at[j]
            size = r.shape[0]
            copies.append(
                pltpu.make_async_copy(r, held.at[pl.ds(start, size)], sems.at[len(copies)])
            )
            copies[-1].start()
            start += size
    values = []
    for k in range(uv_ref.shape[0]):
        context = by_ref[:, k].astype(jnp.float32).reshape(-1, by_ref.shape[3])
        values.append(
            jnp.dot(context.astype(jnp.bfloat16), uv_ref[k], preferred_element_type=jnp.float32)
        )
    values = jnp.concatenate(values, axis=1).astype(jnp.bfloat16)
    x = jnp.dot(select_ref[...], values, preferred_element_type=jnp.float32).astype(jnp.bfloat16)
    half = slots_ref.shape[0]
    each = rows_ref.shape[1]
    first = place_ref[1] == 0
    at, start = 0, 0
    width = held.shape[0] // chips
    core_width = width // 2
    leaving = []
    for k, (ours, theirs) in enumerate(layout):
        for _ in ours + theirs:
            copies[at].wait()
            at += 1
        pair = [
            lax.dot_general(
                x,
                held[start + c * core_width : start + (c + 1) * core_width],
                NT,
                preferred_element_type=jnp.float32,
            )
            for c in range(2)
        ]
        start += width
        whole = jnp.concatenate(
            [jnp.where(first, pair[0], pair[1]), jnp.where(first, pair[1], pair[0])], axis=1
        )
        chip = lax.rem(place_ref[0] + (chips - k), chips)
        columns = pl.ds(pl.multiple_of(chip * width, 128), width)
        carried = jnp.dot(own_ref[...], hidden_ref[:, columns], preferred_element_type=jnp.float32)
        slots_ref[:, columns] = (whole[:half] + carried).astype(jnp.bfloat16)
        for j in range(rows_ref.shape[0]):
            row = half + j * each
            rows_ref[j, :, columns] = whole[row : row + each].astype(jnp.bfloat16)
        for j, out_ref in enumerate(outs):
            source = slots_ref if j == 0 else rows_ref.at[j - 1]
            leaving.append(
                pltpu.make_async_copy(
                    source.at[:, columns], out_ref.at[:, columns], out_sems.at[j, k]
                )
            )
            leaving[-1].start()
    for copy in leaving:
        copy.wait()


def project(place, by_head, w_uv, select, blocks, layout, chooser, hidden, outer, inner):
    rows, depth = select.shape[0], blocks[0].shape[1]
    half = rows // 2
    width = sum(part.size for part in blocks) // depth
    parts = sum(len(a) + len(b) for a, b in layout)
    each = half // inner
    vmem = pl.BlockSpec(memory_space=pltpu.VMEM)
    anywhere = pl.BlockSpec(memory_space=pltpu.HBM)
    return pl.pallas_call(
        functools.partial(project_body, layout),
        in_specs=[pl.BlockSpec(memory_space=pltpu.SMEM)] + [vmem] * 5 + [anywhere] * len(blocks),
        out_specs=[anywhere] * (1 + inner),
        out_shape=[jax.ShapeDtypeStruct((half, width), jnp.bfloat16)]
        + [jax.ShapeDtypeStruct((each, width), jnp.bfloat16)] * inner,
        scratch_shapes=[
            pltpu.VMEM((width, depth), jnp.bfloat16),
            pltpu.VMEM((half, width), jnp.bfloat16),
            pltpu.VMEM((inner, each, width), jnp.bfloat16),
            pltpu.SemaphoreType.DMA((parts,)),
            pltpu.SemaphoreType.DMA((1 + inner, len(layout))),
        ],
        compiler_params=pltpu.CompilerParams(vmem_limit_bytes=63200000),
        cost_estimate=pl.CostEstimate(
            flops=2 * rows * depth * width,
            bytes_accessed=2 * depth * width + 2 * rows * width,
            transcendentals=0,
        ),
        name="project",
    )(place, by_head, w_uv, select, chooser, hidden, *blocks)


def norm_body(parts_ref, gain_ref, *refs):
    total, out_ref = refs[-1], refs[(len(refs) - 2) // 2]
    parts, _, width = parts_ref.shape
    tile = width // 8
    squares = 0.0
    for k in range(8):
        at = slice(k * tile, (k + 1) * tile)
        here = parts_ref[0, :, at].astype(jnp.float32)
        for j in range(1, parts):
            here += parts_ref[j, :, at].astype(jnp.float32)
        total[:, at] = here
        squares += jnp.sum(here * here, axis=1, keepdims=True)
    scale = lax.rsqrt(squares * (1.0 / width) + 1e-06)
    for k in range(8):
        at = slice(k * tile, (k + 1) * tile)
        out_ref[:, at] = (total[:, at] * scale * gain_ref[:, at]).astype(jnp.bfloat16)


def norm(parts, gain, held):
    _, rows, width = parts.shape
    vmem = pl.BlockSpec(memory_space=pltpu.VMEM)
    anywhere = pl.BlockSpec(memory_space=pltpu.HBM)
    return pl.pallas_call(
        norm_body,
        in_specs=[vmem, vmem] + [anywhere] * len(held),
        out_specs=[vmem] + [anywhere] * len(held),
        out_shape=[jax.ShapeDtypeStruct((rows, width), jnp.bfloat16)]
        + [jax.ShapeDtypeStruct(h.shape, h.dtype) for h in held],
        scratch_shapes=[pltpu.VMEM((rows, width), jnp.float32)],
        input_output_aliases={2 + k: 1 + k for k in range(len(held))},
        compiler_params=pltpu.CompilerParams(vmem_limit_bytes=16 * 1024 * 1024),
        cost_estimate=pl.CostEstimate(
            flops=2 * parts.size, bytes_accessed=2 * parts.size, transcendentals=0
        ),
        name="norm",
    )(parts, gain, *held)


def gate_up_body(core_ref, x_ref, own_ref, other_ref, active_ref, gate, up):
    step = pl.program_id(0)

    @pl.when(step == 0)
    def _():
        gate[...] = jnp.zeros_like(gate)
        up[...] = jnp.zeros_like(up)

    x = x_ref[...]
    for part, total in ((0, gate), (1, up)):
        both = jnp.concatenate([own_ref[part], other_ref[part]], axis=1)
        total[...] += jnp.dot(x, both, preferred_element_type=jnp.float32)

    @pl.when(step == pl.num_programs(0) - 1)
    def _():
        g = gate[...]
        active = (g * jax.nn.sigmoid(g) * up[...]).astype(jnp.bfloat16)
        units = active.shape[1] // 2
        first, second = active[:, :units], active[:, units:]

        @pl.when(core_ref[0] == 0)
        def _():
            for k in range(active_ref.shape[0]):
                active_ref[k, :, :units] = first
                active_ref[k, :, units:] = second

        @pl.when(core_ref[0] != 0)
        def _():
            for k in range(active_ref.shape[0]):
                active_ref[k, :, :units] = second
                active_ref[k, :, units:] = first


def gate_up(core, x, own, other, copies):
    rows, depth = x.shape
    units = own.shape[2]
    tile = depth // 4
    return pl.pallas_call(
        gate_up_body,
        grid=(depth // tile,),
        in_specs=[
            pl.BlockSpec(memory_space=pltpu.SMEM),
            pl.BlockSpec((rows, tile), lambda i: (0, i)),
            pl.BlockSpec((2, tile, units), lambda i: (0, i, 0)),
            pl.BlockSpec((2, tile, units), lambda i: (0, i, 0)),
        ],
        out_specs=pl.BlockSpec((copies, rows, 2 * units), lambda i: (0, 0, 0)),
        out_shape=jax.ShapeDtypeStruct((copies, rows, 2 * units), jnp.bfloat16),
        scratch_shapes=[pltpu.VMEM((rows, 2 * units), jnp.float32)] * 2,
        compiler_params=pltpu.CompilerParams(vmem_limit_bytes=24 * 1024 * 1024),
        cost_estimate=pl.CostEstimate(
            flops=8 * rows * depth * units,
            bytes_accessed=8 * depth * units + 2 * rows * depth,
            transcendentals=2 * rows * units,
        ),
        name="gate_up",
    )(core, x, own, other)


def down_body(core_ref, x_ref, own_ref, other_ref, *refs):
    out_ref = refs[-1]
    x = jnp.concatenate([x_ref[k] for k in range(x_ref.shape[0])], axis=1)
    half = own_ref.shape[0]
    parts, each = out_ref.shape[0], out_ref.shape[1]
    mine = lax.dot_general(x, own_ref[...], NT, preferred_element_type=jnp.float32)
    others = lax.dot_general(x, other_ref[...], NT, preferred_element_type=jnp.float32)

    def write(first, second):
        both = jnp.concatenate([first, second], axis=1).reshape(parts, each, 2 * half)
        out_ref[...] = both.astype(jnp.bfloat16)

    @pl.when(core_ref[0] == 0)
    def _():
        write(mine, others)

    @pl.when(core_ref[0] != 0)
    def _():
        write(others, mine)


def down_project(core, x, own, other, *ready):
    parts, rows, _ = x.shape
    columns = 2 * own.shape[0]
    vmem = pl.BlockSpec(memory_space=pltpu.VMEM)
    return pl.pallas_call(
        down_body,
        in_specs=[
            pl.BlockSpec(memory_space=pltpu.SMEM),
            vmem,
            vmem,
            vmem,
            *[pl.BlockSpec(memory_space=pltpu.HBM)] * len(ready),
        ],
        out_specs=vmem,
        out_shape=jax.ShapeDtypeStruct((parts, rows // parts, columns), jnp.bfloat16),
        compiler_params=pltpu.CompilerParams(vmem_limit_bytes=24 * 1024 * 1024),
        cost_estimate=pl.CostEstimate(
            flops=2 * rows * own.shape[1] * columns,
            bytes_accessed=2 * own.shape[1] * columns,
            transcendentals=0,
        ),
        name="down_project",
    )(core, x, own, other, *ready)


def combine_body(count, spread_ref, hidden_ref, *refs):
    blocks, sums, (here_ref, *away) = refs[:count], refs[count : 2 * count], refs[2 * count :]
    weight = spread_ref[...]
    high = weight.astype(jnp.bfloat16)
    low = (weight - high.astype(jnp.float32)).astype(jnp.bfloat16)
    parts, _, width = blocks[0].shape
    each = here_ref.shape[0]
    for k in range(parts):
        slots = jnp.concatenate([b[k].astype(jnp.float32) for b in blocks], axis=0)
        slots = slots.astype(jnp.bfloat16)
        mixed = jnp.dot(high, slots, preferred_element_type=jnp.float32) + jnp.dot(
            low, slots, preferred_element_type=jnp.float32
        )
        at = slice(k * width, (k + 1) * width)
        for r in sums:
            mixed += r[:, at].astype(jnp.float32)
        for y in range(1 + len(away)):
            row = mixed[y * each : (y + 1) * each]
            if y == 0:
                here_ref[:, at] = row + hidden_ref[:, at].astype(jnp.float32)
            else:
                away[y - 1][:, at] = row.astype(jnp.bfloat16)


def combine(spread, hidden, blocks, sums):
    each, width = hidden.shape
    outer = spread.shape[0] // each
    vmem = pl.BlockSpec(memory_space=pltpu.VMEM)
    away = jax.ShapeDtypeStruct((each, width), jnp.bfloat16)
    return pl.pallas_call(
        functools.partial(combine_body, len(blocks)),
        in_specs=[vmem] * (2 + len(blocks) + len(sums)),
        out_specs=[vmem] * outer,
        out_shape=[jax.ShapeDtypeStruct((each, width), jnp.float32)] + [away] * (outer - 1),
        compiler_params=pltpu.CompilerParams(vmem_limit_bytes=16 * 1024 * 1024),
        cost_estimate=pl.CostEstimate(
            flops=4 * spread.shape[0] * spread.shape[1] * width,
            bytes_accessed=10 * spread.shape[0] * width,
            transcendentals=0,
        ),
        name="combine",
    )(spread, hidden, *blocks, *sums)


def shifted(x, axis, by):
    size = lax.axis_size(axis)
    return lax.ppermute(x, axis, [(i, (i + by) % size) for i in range(size)])


def swap_cores(x):
    return lax.ppermute(x, "core", [(0, 1), (1, 0)])


def per_device(
    hidden_in,
    queries,
    fresh,
    res_cache,
    res_len,
    pre_cache,
    pre_len,
    arrival,
    w_uv,
    w_o,
    norm_gain,
    expert_ids,
    route_weight,
    w_gu,
    w_down,
):
    group, head = ("z", "core"), ("y", "x")
    chips, cores, long, short = (lax.axis_size(a) for a in ("z", "core", "y", "x"))
    groups, columns = chips * cores, long * short
    core, at_y, at_x = (lax.axis_index(a) for a in ("core", "y", "x"))
    group_index = lax.axis_index(group)
    steps, rows_dev, width = hidden_in.shape
    resident = res_cache.shape[0]
    newcomers = rows_dev - resident
    requests = arrival.shape[1]
    own_rows = steps * rows_dev
    slots_dev = steps * CAP

    place = jnp.stack([lax.axis_index("z"), core, at_y, at_x]).astype(jnp.int32)
    gu_other = swap_cores(w_gu[0])
    down = w_down[0].T
    down_other = swap_cores(down)

    places = jnp.arange(requests, dtype=jnp.int32)
    arrival_row = arrival[0]
    claimed = arrival_row[None, :] == places[:, None]
    order = jnp.sum(jnp.where(claimed, places[None, :], 0), axis=1)
    len_sorted = jnp.sum(jnp.where(claimed, pre_len[0][None, :], 0), axis=1)
    new_len = lax.dynamic_slice(len_sorted, (group_index * newcomers,), (newcomers,))
    sorted_cache = jnp.take(pre_cache[0], order, axis=0, mode="clip")
    taken = lax.all_to_all(
        sorted_cache.reshape(groups, newcomers, *sorted_cache.shape[1:]),
        group,
        split_axis=0,
        concat_axis=0,
        tiled=False,
    )
    recent = jnp.swapaxes(jnp.pad(fresh, ((0, 8 - steps), (0, 0), (0, 0))), 0, 1)
    done = attend_resident(res_len, queries, jnp.swapaxes(res_cache, 1, 2), recent)
    hidden_own = hidden_in.reshape(own_rows, width)
    block = w_o.T
    up, down_block, near = after(shifted(block, "z", 1), shifted(block, "z", -1), done, pltpu.VMEM)
    context = attend_new(new_len, queries, taken, recent, done, columns, [gu_other, down_other])
    select, own_chooser, spread = routing(
        place,
        jnp.swapaxes(expert_ids, 1, 2),
        jnp.swapaxes(route_weight, 1, 2),
        long,
        short,
        rows_dev,
        [context, hidden_own],
    )
    up, down_block, mid = after(
        shifted(up, "z", 1), shifted(down_block, "z", -1), context, pltpu.HBM
    )
    far = [shifted(up, "z", 1), shifted(down_block, "z", -1)]
    first, second = halves(*far, select)
    last = [shifted(first, "z", 1), shifted(second, "z", -1)]
    blocks = [block, near, mid, *far, *last]
    places = [[(0, None)], [(1, 0)], [(2, 0)], [(3, None)], [(5, None), (6, None)]]
    places += [[(4, None)], [(2, 1)], [(1, 1)]]
    assert len(places) == chips
    count = len(blocks)
    layout = [(parts, [(i + count, j) for i, j in parts]) for parts in places]
    blocks = blocks + [swap_cores(part) for part in blocks]
    by_head = lax.all_to_all(context, head, split_axis=0, concat_axis=0, tiled=False)
    part_slots, row_here, *row_away = project(
        place, by_head, w_uv, select, blocks, layout, own_chooser, hidden_own, long, short
    )
    slot_parts = lax.all_to_all(
        part_slots.reshape(columns, slots_dev, width), head, 0, 0, tiled=False
    )
    normed, *row_away = norm(slot_parts, norm_gain[None], row_away)
    row_parts = [row_here] + [shifted(r, "x", k + 1) for k, r in enumerate(row_away)]

    core_now = jnp.reshape(core, (1,)).astype(jnp.int32)
    portion = lax.all_gather(normed, "z", axis=0, tiled=True)
    active = gate_up(core_now, portion, w_gu[0], gu_other, chips)
    everywhere = lax.all_to_all(active, "z", 0, 0, tiled=False)
    outcome = down_project(core_now, everywhere, down, down_other, *row_parts[1:])
    slot_values = lax.all_to_all(outcome, "z", 0, 0, tiled=False)
    beside = [slot_values] + [shifted(slot_values, "x", k) for k in range(1, short)]
    out, *mixed = combine(spread, hidden_own, beside, row_parts)
    for k, part in enumerate(mixed):
        out = out + shifted(part, "y", k + 1).astype(jnp.float32)
    return out.astype(jnp.bfloat16).reshape(steps, rows_dev, width)


def solution(mesh):
    wide = Mesh(mesh.devices.reshape(8, 2, 4, 4), ("z", "core", "y", "x"))
    group, head = ("z", "core"), ("y", "x")
    both = group + head
    placed = (
        P(None, both, None),
        P(None, both, None, None),
        P(None, both, None),
        P(both, None, None),
        P(both),
        P(head, None, group, None),
        P(head, None),
        P(head, None),
        P(head, None, None),
        P(head, group),
        P(),
        P(None, group, None),
        P(None, group, None),
        P(head, None, None, group),
        P(head, None, group),
    )
    return jax.shard_map(
        per_device,
        mesh=wide,
        in_specs=placed,
        out_specs=P(None, both, None),
        check_vma=False,
    )
```

```python
import functools

import jax
import jax.numpy as jnp
from jax import lax
from jax.experimental import pallas as pl
from jax.experimental.pallas import tpu as pltpu
from jax.sharding import Mesh
from jax.sharding import PartitionSpec as P

LAT = 512
ROPE = 64
VD = 128
CAP = 4
STEPS = 2


NT = (((1,), (1,)), ((), ()))


def context_of(query, scores, values, fresh, length):
    scaling = (VD + ROPE) ** (-0.5)
    cached = scores(query) * scaling
    places = lax.broadcasted_iota(jnp.int32, cached.shape, 1)
    cached = jnp.where(places < length, cached, -jnp.inf)
    recent = lax.dot_general(query, fresh, NT, preferred_element_type=jnp.float32) * scaling
    step = lax.broadcasted_iota(jnp.int32, recent.shape, 0) // (query.shape[0] // STEPS)
    recent = jnp.where(lax.broadcasted_iota(jnp.int32, recent.shape, 1) <= step, recent, -jnp.inf)
    highest = jnp.maximum(
        jnp.max(cached, axis=1, keepdims=True), jnp.max(recent, axis=1, keepdims=True)
    )
    cached, recent = jnp.exp(cached - highest), jnp.exp(recent - highest)
    totals = jnp.sum(cached, axis=1, keepdims=True) + jnp.sum(recent, axis=1, keepdims=True)
    cached, recent = (cached / totals).astype(jnp.bfloat16), (recent / totals).astype(jnp.bfloat16)
    mixed = values(cached) + jnp.dot(
        recent, fresh[:, :LAT], preferred_element_type=jnp.float32
    )
    return mixed.astype(jnp.bfloat16)


def attend_resident_body(row, len_ref, q_ref, keys_ref, fresh_ref, out_ref):
    keys = keys_ref[0]
    query = jnp.concatenate([q_ref[t, 0] for t in range(STEPS)], axis=0)
    out_ref[0] = context_of(
        query,
        lambda q: jnp.dot(q, keys, preferred_element_type=jnp.float32),
        lambda p: lax.dot_general(p, keys[:LAT], NT, preferred_element_type=jnp.float32),
        fresh_ref[0],
        len_ref[row],
    )


def attend_resident(row, lengths, queries, keys, fresh):
    _, width, places = keys.shape
    steps, _, heads, _ = queries.shape
    return pl.pallas_call(
        functools.partial(attend_resident_body, row),
        grid=(1,),
        in_specs=[
            pl.BlockSpec(memory_space=pltpu.SMEM),
            pl.BlockSpec((steps, 1, heads, width), lambda i: (0, row, 0, 0)),
            pl.BlockSpec((1, width, places), lambda i: (row, 0, 0)),
            pl.BlockSpec((1, *fresh.shape[1:]), lambda i: (row, 0, 0)),
        ],
        out_specs=pl.BlockSpec((1, steps * heads, LAT), lambda i: (0, 0, 0)),
        out_shape=jax.ShapeDtypeStruct((1, steps * heads, LAT), jnp.bfloat16),
        compiler_params=pltpu.CompilerParams(vmem_limit_bytes=24 * 1024 * 1024),
        cost_estimate=pl.CostEstimate(
            flops=4 * width * places * steps * heads, bytes_accessed=10000000, transcendentals=0
        ),
        name="attend_resident",
    )(lengths, queries, keys, fresh)


def attend_new_body(resident, len_ref, q_ref, taken_ref, fresh_ref, *refs):
    out_ref = refs[-1]
    queries = refs[0].shape[1]
    fresh_rows = q_ref.shape[1]
    contexts = [refs[n][0] for n in range(resident)]
    for n in range(fresh_rows):
        keys = taken_ref[:, n].astype(jnp.float32)
        keys = keys.reshape(-1, keys.shape[2]).astype(jnp.bfloat16)
        contexts.append(
            context_of(
                jnp.concatenate([q_ref[t, n] for t in range(STEPS)], axis=0),
                lambda q: lax.dot_general(q, keys, NT, preferred_element_type=jnp.float32),
                lambda p: jnp.dot(p, keys[:, :LAT], preferred_element_type=jnp.float32),
                fresh_ref[n],
                len_ref[n],
            )
        )
    rows = resident + fresh_rows
    context = jnp.concatenate(contexts, axis=0)
    size = context.shape[0]
    heads = queries // STEPS
    to = lax.broadcasted_iota(jnp.int32, (size, size), 0)
    source = to % rows * queries + to // rows % STEPS * heads + to // (rows * STEPS)
    turn = (source == lax.broadcasted_iota(jnp.int32, (size, size), 1)).astype(jnp.float32)
    turned = jnp.dot(turn.astype(jnp.bfloat16), context, preferred_element_type=jnp.float32)
    out_ref[...] = turned.reshape(out_ref.shape).astype(jnp.bfloat16)


def attend_new(lengths, queries, taken, fresh, done, columns, ready):
    _, rows, _, width = taken.shape
    steps, whole, heads, _ = queries.shape
    out = (columns, heads // columns, steps * whole, LAT)
    last = whole // rows - 1
    return pl.pallas_call(
        functools.partial(attend_new_body, len(done)),
        grid=(1,),
        in_specs=[
            pl.BlockSpec(memory_space=pltpu.SMEM),
            pl.BlockSpec((steps, rows, heads, width), lambda i: (0, last, 0, 0)),
            pl.BlockSpec(taken.shape, lambda i: (0, 0, 0, 0)),
            pl.BlockSpec((rows, *fresh.shape[1:]), lambda i: (last, 0, 0)),
            *[pl.BlockSpec(d.shape, lambda i: (0, 0, 0)) for d in done],
        ]
        + [pl.BlockSpec(memory_space=pltpu.HBM)] * len(ready),
        out_specs=pl.BlockSpec(out, lambda i: (0, 0, 0, 0)),
        out_shape=jax.ShapeDtypeStruct(out, jnp.bfloat16),
        compiler_params=pltpu.CompilerParams(vmem_limit_bytes=24 * 1024 * 1024),
        cost_estimate=pl.CostEstimate(
            flops=4 * taken.size * steps * heads, bytes_accessed=20000000, transcendentals=0
        ),
        name="attend_new",
    )(lengths, queries, taken, fresh, *done, *ready)


def picked(one_hot, x, dims=(((1,), (0,)), ((), ()))):
    one_hot = one_hot.astype(jnp.float32).astype(jnp.bfloat16)
    total = None
    for _ in range(3):
        part = x.astype(jnp.bfloat16)
        x = x - part.astype(jnp.float32)
        term = lax.dot_general(one_hot, part, dims, preferred_element_type=jnp.float32)
        total = term if total is None else total + term
    return total


def routing_body(sizes, place_ref, ids_ref, weights_ref, *refs):
    long, short, rows_dev = sizes
    select_ref, own_ref, spread_ref, present_ref, weight_ref = refs[-5:]
    steps, _, rows = ids_ref.shape
    columns = long * short
    own_rows, slots = steps * rows_dev, steps * CAP
    at_y, at_x = place_ref[2], place_ref[3]

    def iota(shape, axis):
        return lax.broadcasted_iota(jnp.int32, shape, axis)

    for t in range(steps):
        ids, weights = ids_ref[t], weights_ref[t]
        for e in range(columns):
            at = slice(e * steps + t, e * steps + t + 1)
            matched = ids == e
            present_ref[at] = jnp.max(matched.astype(jnp.float32), axis=0, keepdims=True)
            weight_ref[at] = jnp.sum(jnp.where(matched, weights, 0.0), axis=0, keepdims=True)
    present = present_ref[...]
    before = iota((rows, rows), 0) < iota((rows, rows), 1)
    place = jnp.dot(
        present.astype(jnp.bfloat16),
        before.astype(jnp.float32).astype(jnp.bfloat16),
        preferred_element_type=jnp.float32,
    )
    count = columns * slots
    widen = iota((count, columns * steps), 0) // CAP == iota((count, columns * steps), 1)
    slot = (iota((count, rows), 0) % CAP).astype(jnp.float32)
    chosen = (picked(widen, place) == slot) & (picked(widen, present) > 0.5)
    weighted = jnp.where(chosen, picked(widen, weight_ref[...]), 0.0)
    total = columns * own_rows
    to = iota((rows, total), 1)
    spot = to // own_rows * rows_dev + to % rows_dev == iota((rows, total), 0)
    same = (
        iota((count, total), 0) // CAP % steps == iota((count, total), 1) // rows_dev % steps
    )
    spot = spot.astype(jnp.float32).astype(jnp.bfloat16)
    chooser = jnp.dot(
        chosen.astype(jnp.float32).astype(jnp.bfloat16), spot, preferred_element_type=jnp.float32
    )
    chooser = jnp.where(same, chooser, 0.0).astype(jnp.bfloat16)
    select_ref[:count] = chooser
    to = iota((total, total), 0)
    from_x = (at_x + to // (long * own_rows)) % short
    from_y = (at_y + to // own_rows % long) % long
    source = (from_y * short + from_x) * own_rows + to % own_rows
    turned = source == iota((total, total), 1)
    select_ref[count:] = turned.astype(jnp.float32).astype(jnp.bfloat16)
    head = at_y * short + at_x
    mine = iota((total, own_rows), 0) == head * own_rows + iota((total, own_rows), 1)
    own_ref[...] = jnp.dot(
        chooser, mine.astype(jnp.float32).astype(jnp.bfloat16), preferred_element_type=jnp.float32
    ).astype(jnp.bfloat16)
    to = iota((short * slots, count), 0)
    expert = at_y * short + (at_x + short - to // slots) % short
    near = picked(expert * slots + to % slots == iota((short * slots, count), 1), weighted)
    to = iota((long * own_rows, rows), 0)
    row = ((at_y + to // own_rows) % long * short + at_x) * rows_dev + to % rows_dev
    near = picked(row == iota((long * own_rows, rows), 1), near, NT)
    shape = (long * own_rows, short * slots)
    same = iota(shape, 0) // rows_dev % steps == iota(shape, 1) // CAP % steps
    spread_ref[...] = jnp.where(same, near, 0.0)


def routing(place, ids, weights, long, short, rows_dev, ready):
    steps, _, rows = ids.shape
    count, total = long * short * steps * CAP, rows * steps
    vmem = pl.BlockSpec(memory_space=pltpu.VMEM)
    return pl.pallas_call(
        functools.partial(routing_body, (long, short, rows_dev)),
        in_specs=[
            pl.BlockSpec(memory_space=pltpu.SMEM),
            vmem,
            vmem,
            *[pl.BlockSpec(memory_space=pltpu.HBM)] * len(ready),
        ],
        out_specs=[vmem] * 3,
        out_shape=[
            jax.ShapeDtypeStruct((count + total, total), jnp.bfloat16),
            jax.ShapeDtypeStruct((count, steps * rows_dev), jnp.bfloat16),
            jax.ShapeDtypeStruct((long * steps * rows_dev, short * steps * CAP), jnp.float32),
        ],
        scratch_shapes=[pltpu.VMEM((long * short * steps, rows), jnp.float32)] * 2,
        compiler_params=pltpu.CompilerParams(vmem_limit_bytes=24 * 1024 * 1024),
        cost_estimate=pl.CostEstimate(flops=0, bytes_accessed=100000, transcendentals=0),
        name="routing",
    )(place, ids, weights, *ready)


def after_body(up_ref, down_ref, ready_ref, out_up_ref, out_down_ref, pair_ref):
    del ready_ref
    for k, (ref, out_ref) in enumerate([(up_ref, out_up_ref), (down_ref, out_down_ref)]):
        block = ref[...]
        out_ref[...] = block
        pair_ref[k] = block


def after(up, down, ready, space):
    vmem = pl.BlockSpec(memory_space=pltpu.VMEM)
    one = jax.ShapeDtypeStruct(up.shape, up.dtype)
    return pl.pallas_call(
        after_body,
        in_specs=[vmem, vmem, pl.BlockSpec(memory_space=space)],
        out_specs=[vmem] * 3,
        out_shape=[one, one, jax.ShapeDtypeStruct((2, *up.shape), up.dtype)],
        compiler_params=pltpu.CompilerParams(vmem_limit_bytes=8 * 1024 * 1024),
        cost_estimate=pl.CostEstimate(flops=0, bytes_accessed=100000, transcendentals=0),
        name="after",
    )(up, down, ready)


def halves_body(up_ref, down_ref, ready_ref, first_ref, second_ref):
    del ready_ref
    half = first_ref.shape[0]
    first_ref[...] = up_ref[:half]
    second_ref[...] = down_ref[half:]


def halves(up, down, ready):
    vmem = pl.BlockSpec(memory_space=pltpu.VMEM)
    half = jax.ShapeDtypeStruct((up.shape[0] // 2, up.shape[1]), up.dtype)
    return pl.pallas_call(
        halves_body,
        in_specs=[vmem] * 3,
        out_specs=[vmem] * 2,
        out_shape=[half, half],
        compiler_params=pltpu.CompilerParams(vmem_limit_bytes=8 * 1024 * 1024),
        cost_estimate=pl.CostEstimate(flops=0, bytes_accessed=100000, transcendentals=0),
        name="halves",
    )(up, down, ready)


def project_body(layout, place_ref, by_ref, uv_ref, select_ref, own_ref, hidden_ref, *refs):
    total = 1 + max(i for pair in layout for parts in pair for i, _ in parts)
    blocks, outs = refs[:total], refs[total:-5]
    held, slots_ref, rows_ref, sems, out_sems = refs[-5:]
    chips = len(layout)
    copies, start = [], 0
    for pair in layout:
        for i, j in pair[0] + pair[1]:
            r = blocks[i] if j is None else blocks[i].at[j]
            size = r.shape[0]
            copies.append(
                pltpu.make_async_copy(r, held.at[pl.ds(start, size)], sems.at[len(copies)])
            )
            copies[-1].start()
            start += size
    values = []
    for k in range(uv_ref.shape[0]):
        context = by_ref[:, k].astype(jnp.float32).reshape(-1, by_ref.shape[3])
        values.append(
            jnp.dot(context.astype(jnp.bfloat16), uv_ref[k], preferred_element_type=jnp.float32)
        )
    values = jnp.concatenate(values, axis=1).astype(jnp.bfloat16)
    x = jnp.dot(select_ref[...], values, preferred_element_type=jnp.float32).astype(jnp.bfloat16)
    half = slots_ref.shape[0]
    each = rows_ref.shape[1]
    first = place_ref[1] == 0
    at, start = 0, 0
    width = held.shape[0] // chips
    core_width = width // 2
    leaving = []
    for k, (ours, theirs) in enumerate(layout):
        for _ in ours + theirs:
            copies[at].wait()
            at += 1
        pair = [
            lax.dot_general(
                x,
                held[start + c * core_width : start + (c + 1) * core_width],
                NT,
                preferred_element_type=jnp.float32,
            )
            for c in range(2)
        ]
        start += width
        whole = jnp.concatenate(
            [jnp.where(first, pair[0], pair[1]), jnp.where(first, pair[1], pair[0])], axis=1
        )
        chip = lax.rem(place_ref[0] + (chips - k), chips)
        columns = pl.ds(pl.multiple_of(chip * width, 128), width)
        carried = jnp.dot(own_ref[...], hidden_ref[:, columns], preferred_element_type=jnp.float32)
        slots_ref[:, columns] = (whole[:half] + carried).astype(jnp.bfloat16)
        for j in range(rows_ref.shape[0]):
            row = half + j * each
            rows_ref[j, :, columns] = whole[row : row + each].astype(jnp.bfloat16)
        for j, out_ref in enumerate(outs):
            source = slots_ref if j == 0 else rows_ref.at[j - 1]
            leaving.append(
                pltpu.make_async_copy(
                    source.at[:, columns], out_ref.at[:, columns], out_sems.at[j, k]
                )
            )
            leaving[-1].start()
    for copy in leaving:
        copy.wait()


def project(place, by_head, w_uv, select, blocks, layout, chooser, hidden, outer, inner):
    rows, depth = select.shape[0], blocks[0].shape[1]
    half = rows // 2
    width = sum(part.size for part in blocks) // depth
    parts = sum(len(a) + len(b) for a, b in layout)
    each = half // inner
    vmem = pl.BlockSpec(memory_space=pltpu.VMEM)
    anywhere = pl.BlockSpec(memory_space=pltpu.HBM)
    return pl.pallas_call(
        functools.partial(project_body, layout),
        in_specs=[pl.BlockSpec(memory_space=pltpu.SMEM)] + [vmem] * 5 + [anywhere] * len(blocks),
        out_specs=[anywhere] * (1 + inner),
        out_shape=[jax.ShapeDtypeStruct((half, width), jnp.bfloat16)]
        + [jax.ShapeDtypeStruct((each, width), jnp.bfloat16)] * inner,
        scratch_shapes=[
            pltpu.VMEM((width, depth), jnp.bfloat16),
            pltpu.VMEM((half, width), jnp.bfloat16),
            pltpu.VMEM((inner, each, width), jnp.bfloat16),
            pltpu.SemaphoreType.DMA((parts,)),
            pltpu.SemaphoreType.DMA((1 + inner, len(layout))),
        ],
        compiler_params=pltpu.CompilerParams(vmem_limit_bytes=63200000),
        cost_estimate=pl.CostEstimate(
            flops=2 * rows * depth * width,
            bytes_accessed=2 * depth * width + 2 * rows * width,
            transcendentals=0,
        ),
        name="project",
    )(place, by_head, w_uv, select, chooser, hidden, *blocks)


def norm_body(parts_ref, gain_ref, *refs):
    total, out_ref = refs[-1], refs[(len(refs) - 2) // 2]
    parts, _, width = parts_ref.shape
    tile = width // 8
    squares = 0.0
    for k in range(8):
        at = slice(k * tile, (k + 1) * tile)
        here = parts_ref[0, :, at].astype(jnp.float32)
        for j in range(1, parts):
            here += parts_ref[j, :, at].astype(jnp.float32)
        total[:, at] = here
        squares += jnp.sum(here * here, axis=1, keepdims=True)
    scale = lax.rsqrt(squares * (1.0 / width) + 1e-06)
    for k in range(8):
        at = slice(k * tile, (k + 1) * tile)
        out_ref[:, at] = (total[:, at] * scale * gain_ref[:, at]).astype(jnp.bfloat16)


def norm(parts, gain, held):
    _, rows, width = parts.shape
    vmem = pl.BlockSpec(memory_space=pltpu.VMEM)
    anywhere = pl.BlockSpec(memory_space=pltpu.HBM)
    return pl.pallas_call(
        norm_body,
        in_specs=[vmem, vmem] + [anywhere] * len(held),
        out_specs=[vmem] + [anywhere] * len(held),
        out_shape=[jax.ShapeDtypeStruct((rows, width), jnp.bfloat16)]
        + [jax.ShapeDtypeStruct(h.shape, h.dtype) for h in held],
        scratch_shapes=[pltpu.VMEM((rows, width), jnp.float32)],
        input_output_aliases={2 + k: 1 + k for k in range(len(held))},
        compiler_params=pltpu.CompilerParams(vmem_limit_bytes=16 * 1024 * 1024),
        cost_estimate=pl.CostEstimate(
            flops=2 * parts.size, bytes_accessed=2 * parts.size, transcendentals=0
        ),
        name="norm",
    )(parts, gain, *held)


def gate_up_body(core_ref, x_ref, own_ref, other_ref, *refs):
    active_ref, gate, up = refs[-3:]
    step = pl.program_id(0)

    @pl.when(step == 0)
    def _():
        gate[...] = jnp.zeros_like(gate)
        up[...] = jnp.zeros_like(up)

    x = x_ref[...]
    for part, total in ((0, gate), (1, up)):
        both = jnp.concatenate([own_ref[part], other_ref[part]], axis=1)
        total[...] += jnp.dot(x, both, preferred_element_type=jnp.float32)

    @pl.when(step == pl.num_programs(0) - 1)
    def _():
        g = gate[...]
        active = (g * jax.nn.sigmoid(g) * up[...]).astype(jnp.bfloat16)
        units = active.shape[1] // 2
        first, second = active[:, :units], active[:, units:]

        @pl.when(core_ref[0] == 0)
        def _():
            for k in range(active_ref.shape[0]):
                active_ref[k, :, :units] = first
                active_ref[k, :, units:] = second

        @pl.when(core_ref[0] != 0)
        def _():
            for k in range(active_ref.shape[0]):
                active_ref[k, :, :units] = second
                active_ref[k, :, units:] = first


def gate_up(core, x, own, other, copies, ready):
    rows, depth = x.shape
    units = own.shape[2]
    tile = depth // 4
    return pl.pallas_call(
        gate_up_body,
        grid=(depth // tile,),
        in_specs=[
            pl.BlockSpec(memory_space=pltpu.SMEM),
            pl.BlockSpec((rows, tile), lambda i: (0, i)),
            pl.BlockSpec((2, tile, units), lambda i: (0, i, 0)),
            pl.BlockSpec((2, tile, units), lambda i: (0, i, 0)),
            *[pl.BlockSpec(memory_space=pltpu.HBM)] * len(ready),
        ],
        out_specs=pl.BlockSpec((copies, rows, 2 * units), lambda i: (0, 0, 0)),
        out_shape=jax.ShapeDtypeStruct((copies, rows, 2 * units), jnp.bfloat16),
        scratch_shapes=[pltpu.VMEM((rows, 2 * units), jnp.float32)] * 2,
        compiler_params=pltpu.CompilerParams(vmem_limit_bytes=24 * 1024 * 1024),
        cost_estimate=pl.CostEstimate(
            flops=8 * rows * depth * units,
            bytes_accessed=8 * depth * units + 2 * rows * depth,
            transcendentals=2 * rows * units,
        ),
        name="gate_up",
    )(core, x, own, other, *ready)


def down_body(core_ref, x_ref, own_ref, other_ref, out_ref):
    x = jnp.concatenate([x_ref[k] for k in range(x_ref.shape[0])], axis=1)
    half = own_ref.shape[0]
    parts, each = out_ref.shape[0], out_ref.shape[1]
    mine = lax.dot_general(x, own_ref[...], NT, preferred_element_type=jnp.float32)
    others = lax.dot_general(x, other_ref[...], NT, preferred_element_type=jnp.float32)

    def write(first, second):
        both = jnp.concatenate([first, second], axis=1).reshape(parts, each, 2 * half)
        out_ref[...] = both.astype(jnp.bfloat16)

    @pl.when(core_ref[0] == 0)
    def _():
        write(mine, others)

    @pl.when(core_ref[0] != 0)
    def _():
        write(others, mine)


def down_project(core, x, own, other):
    parts, rows, _ = x.shape
    columns = 2 * own.shape[0]
    vmem = pl.BlockSpec(memory_space=pltpu.VMEM)
    return pl.pallas_call(
        down_body,
        in_specs=[
            pl.BlockSpec(memory_space=pltpu.SMEM),
            vmem,
            vmem,
            vmem,
        ],
        out_specs=vmem,
        out_shape=jax.ShapeDtypeStruct((parts, rows // parts, columns), jnp.bfloat16),
        compiler_params=pltpu.CompilerParams(vmem_limit_bytes=24 * 1024 * 1024),
        cost_estimate=pl.CostEstimate(
            flops=2 * rows * own.shape[1] * columns,
            bytes_accessed=2 * own.shape[1] * columns,
            transcendentals=0,
        ),
        name="down_project",
    )(core, x, own, other)


def combine_body(count, spread_ref, hidden_ref, *refs):
    blocks, sums, (here_ref, *away) = refs[:count], refs[count : 2 * count], refs[2 * count :]
    weight = spread_ref[...]
    high = weight.astype(jnp.bfloat16)
    low = (weight - high.astype(jnp.float32)).astype(jnp.bfloat16)
    parts, _, width = blocks[0].shape
    each = here_ref.shape[0]
    for k in range(parts):
        slots = jnp.concatenate([b[k].astype(jnp.float32) for b in blocks], axis=0)
        slots = slots.astype(jnp.bfloat16)
        mixed = jnp.dot(high, slots, preferred_element_type=jnp.float32) + jnp.dot(
            low, slots, preferred_element_type=jnp.float32
        )
        at = slice(k * width, (k + 1) * width)
        for r in sums:
            mixed += r[:, at].astype(jnp.float32)
        for y in range(1 + len(away)):
            row = mixed[y * each : (y + 1) * each]
            if y == 0:
                here_ref[:, at] = row + hidden_ref[:, at].astype(jnp.float32)
            else:
                away[y - 1][:, at] = row.astype(jnp.bfloat16)


def combine(spread, hidden, blocks, sums):
    each, width = hidden.shape
    outer = spread.shape[0] // each
    vmem = pl.BlockSpec(memory_space=pltpu.VMEM)
    away = jax.ShapeDtypeStruct((each, width), jnp.bfloat16)
    return pl.pallas_call(
        functools.partial(combine_body, len(blocks)),
        in_specs=[vmem] * (2 + len(blocks) + len(sums)),
        out_specs=[vmem] * outer,
        out_shape=[jax.ShapeDtypeStruct((each, width), jnp.float32)] + [away] * (outer - 1),
        compiler_params=pltpu.CompilerParams(vmem_limit_bytes=16 * 1024 * 1024),
        cost_estimate=pl.CostEstimate(
            flops=4 * spread.shape[0] * spread.shape[1] * width,
            bytes_accessed=10 * spread.shape[0] * width,
            transcendentals=0,
        ),
        name="combine",
    )(spread, hidden, *blocks, *sums)


def finish_body(here_ref, *refs):
    *parts, out_ref = refs
    total = here_ref[...]
    for r in parts:
        total += r[...].astype(jnp.float32)
    steps, rows, _ = out_ref.shape
    for t in range(steps):
        out_ref[t] = total[t * rows : (t + 1) * rows].astype(jnp.bfloat16)


def finish(here, parts, steps):
    rows, width = here.shape
    vmem = pl.BlockSpec(memory_space=pltpu.VMEM)
    return pl.pallas_call(
        finish_body,
        in_specs=[vmem] * (1 + len(parts)),
        out_specs=vmem,
        out_shape=jax.ShapeDtypeStruct((steps, rows // steps, width), jnp.bfloat16),
        compiler_params=pltpu.CompilerParams(vmem_limit_bytes=8 * 1024 * 1024),
        name="finish",
    )(here, *parts)


def shifted(x, axis, by):
    size = lax.axis_size(axis)
    return lax.ppermute(x, axis, [(i, (i + by) % size) for i in range(size)])


def swap_cores(x):
    return lax.ppermute(x, "core", [(0, 1), (1, 0)])


def per_device(
    hidden_in,
    queries,
    fresh,
    res_cache,
    res_len,
    pre_cache,
    pre_len,
    arrival,
    w_uv,
    w_o,
    norm_gain,
    expert_ids,
    route_weight,
    w_gu,
    w_down,
):
    group, head = ("z", "core"), ("y", "x")
    chips, cores, long, short = (lax.axis_size(a) for a in ("z", "core", "y", "x"))
    groups, columns = chips * cores, long * short
    core, at_y, at_x = (lax.axis_index(a) for a in ("core", "y", "x"))
    group_index = lax.axis_index(group)
    steps, rows_dev, width = hidden_in.shape
    resident = res_cache.shape[0]
    newcomers = rows_dev - resident
    requests = arrival.shape[1]
    own_rows = steps * rows_dev
    slots_dev = steps * CAP

    place = jnp.stack([lax.axis_index("z"), core, at_y, at_x]).astype(jnp.int32)
    gu_other = swap_cores(w_gu[0])
    down = w_down[0].T
    down_other = swap_cores(down)

    places = jnp.arange(requests, dtype=jnp.int32)
    arrival_row = arrival[0]
    claimed = arrival_row[None, :] == places[:, None]
    order = jnp.sum(jnp.where(claimed, places[None, :], 0), axis=1)
    len_sorted = jnp.sum(jnp.where(claimed, pre_len[0][None, :], 0), axis=1)
    new_len = lax.dynamic_slice(len_sorted, (group_index * newcomers,), (newcomers,))
    sorted_cache = jnp.take(pre_cache[0], order, axis=0, mode="clip")
    taken = lax.all_to_all(
        sorted_cache.reshape(groups, newcomers, *sorted_cache.shape[1:]),
        group,
        split_axis=0,
        concat_axis=0,
        tiled=False,
    )
    recent = jnp.swapaxes(jnp.pad(fresh, ((0, 8 - steps), (0, 0), (0, 0))), 0, 1)
    by_width = jnp.swapaxes(res_cache, 1, 2)
    done = [attend_resident(k, res_len, queries, by_width, recent) for k in range(resident)]
    hidden_own = hidden_in.reshape(own_rows, width)
    block = w_o.T
    up, down_block, near = after(shifted(block, "z", 1), shifted(block, "z", -1), done[0], pltpu.VMEM)
    context = attend_new(new_len, queries, taken, recent, done, columns, [gu_other, down_other])
    select, own_chooser, spread = routing(
        place,
        jnp.swapaxes(expert_ids, 1, 2),
        jnp.swapaxes(route_weight, 1, 2),
        long,
        short,
        rows_dev,
        [context, hidden_own],
    )
    up, down_block, mid = after(
        shifted(up, "z", 1), shifted(down_block, "z", -1), context, pltpu.HBM
    )
    far = [shifted(up, "z", 1), shifted(down_block, "z", -1)]
    first, second = halves(*far, select)
    last = [shifted(first, "z", 1), shifted(second, "z", -1)]
    blocks = [block, near, mid, *far, *last]
    places = [[(0, None)], [(1, 0)], [(2, 0)], [(3, None)], [(5, None), (6, None)]]
    places += [[(4, None)], [(2, 1)], [(1, 1)]]
    assert len(places) == chips
    count = len(blocks)
    layout = [(parts, [(i + count, j) for i, j in parts]) for parts in places]
    blocks = blocks + [swap_cores(part) for part in blocks]
    by_head = lax.all_to_all(context, head, split_axis=0, concat_axis=0, tiled=False)
    part_slots, row_here, *row_away = project(
        place, by_head, w_uv, select, blocks, layout, own_chooser, hidden_own, long, short
    )
    slot_parts = lax.all_to_all(
        part_slots.reshape(columns, slots_dev, width), head, 0, 0, tiled=False
    )
    normed, *row_away = norm(slot_parts, norm_gain[None], row_away)
    row_parts = [row_here] + [shifted(r, "x", k + 1) for k, r in enumerate(row_away)]

    core_now = jnp.reshape(core, (1,)).astype(jnp.int32)
    portion = lax.all_gather(normed, "z", axis=0, tiled=True)
    active = gate_up(core_now, portion, w_gu[0], gu_other, chips, row_parts[1:])
    everywhere = lax.all_to_all(active, "z", 0, 0, tiled=False)
    outcome = down_project(core_now, everywhere, down, down_other)
    slot_values = lax.all_to_all(outcome, "z", 0, 0, tiled=False)
    beside = [slot_values] + [shifted(slot_values, "x", k) for k in range(1, short)]
    out, *mixed = combine(spread, hidden_own, beside, row_parts)
    return finish(out, [shifted(part, "y", k + 1) for k, part in enumerate(mixed)], steps)


def solution(mesh):
    wide = Mesh(mesh.devices.reshape(8, 2, 4, 4), ("z", "core", "y", "x"))
    group, head = ("z", "core"), ("y", "x")
    both = group + head
    placed = (
        P(None, both, None),
        P(None, both, None, None),
        P(None, both, None),
        P(both, None, None),
        P(both),
        P(head, None, group, None),
        P(head, None),
        P(head, None),
        P(head, None, None),
        P(head, group),
        P(),
        P(None, group, None),
        P(None, group, None),
        P(head, None, None, group),
        P(head, None, group),
    )
    return jax.shard_map(
        per_device,
        mesh=wide,
        in_specs=placed,
        out_specs=P(None, both, None),
        check_vma=False,
    )
```

```python
import functools

import jax
import jax.numpy as jnp
from jax import lax
from jax.experimental import pallas as pl
from jax.experimental.pallas import tpu as pltpu
from jax.sharding import Mesh
from jax.sharding import PartitionSpec as P

LAT = 512
ROPE = 64
VD = 128
CAP = 4
STEPS = 2


NT = (((1,), (1,)), ((), ()))


def context_of(query, scores, values, fresh, length):
    scaling = (VD + ROPE) ** (-0.5)
    cached = scores(query) * scaling
    places = lax.broadcasted_iota(jnp.int32, cached.shape, 1)
    cached = jnp.where(places < length, cached, -jnp.inf)
    recent = lax.dot_general(query, fresh, NT, preferred_element_type=jnp.float32) * scaling
    step = lax.broadcasted_iota(jnp.int32, recent.shape, 0) // (query.shape[0] // STEPS)
    recent = jnp.where(lax.broadcasted_iota(jnp.int32, recent.shape, 1) <= step, recent, -jnp.inf)
    highest = jnp.maximum(
        jnp.max(cached, axis=1, keepdims=True), jnp.max(recent, axis=1, keepdims=True)
    )
    cached, recent = jnp.exp(cached - highest), jnp.exp(recent - highest)
    totals = jnp.sum(cached, axis=1, keepdims=True) + jnp.sum(recent, axis=1, keepdims=True)
    cached, recent = (cached / totals).astype(jnp.bfloat16), (recent / totals).astype(jnp.bfloat16)
    mixed = values(cached) + jnp.dot(
        recent, fresh[:, :LAT], preferred_element_type=jnp.float32
    )
    return mixed.astype(jnp.bfloat16)


def attend_resident_body(row, len_ref, q_ref, keys_ref, fresh_ref, out_ref):
    keys = keys_ref[0]
    query = jnp.concatenate([q_ref[t, 0] for t in range(STEPS)], axis=0)
    out_ref[0] = context_of(
        query,
        lambda q: jnp.dot(q, keys, preferred_element_type=jnp.float32),
        lambda p: lax.dot_general(p, keys[:LAT], NT, preferred_element_type=jnp.float32),
        fresh_ref[0],
        len_ref[row],
    )


def attend_resident(row, lengths, queries, keys, fresh):
    _, width, places = keys.shape
    steps, _, heads, _ = queries.shape
    return pl.pallas_call(
        functools.partial(attend_resident_body, row),
        grid=(1,),
        in_specs=[
            pl.BlockSpec(memory_space=pltpu.SMEM),
            pl.BlockSpec((steps, 1, heads, width), lambda i: (0, row, 0, 0)),
            pl.BlockSpec((1, width, places), lambda i: (row, 0, 0)),
            pl.BlockSpec((1, *fresh.shape[1:]), lambda i: (row, 0, 0)),
        ],
        out_specs=pl.BlockSpec((1, steps * heads, LAT), lambda i: (0, 0, 0)),
        out_shape=jax.ShapeDtypeStruct((1, steps * heads, LAT), jnp.bfloat16),
        compiler_params=pltpu.CompilerParams(vmem_limit_bytes=24 * 1024 * 1024),
        cost_estimate=pl.CostEstimate(
            flops=4 * width * places * steps * heads, bytes_accessed=10000000, transcendentals=0
        ),
        name="attend_resident",
    )(lengths, queries, keys, fresh)


def attend_new_body(resident, len_ref, q_ref, taken_ref, fresh_ref, *refs):
    out_ref = refs[-1]
    queries = refs[0].shape[1]
    fresh_rows = q_ref.shape[1]
    contexts = [refs[n][0] for n in range(resident)]
    for n in range(fresh_rows):
        keys = taken_ref[:, n].astype(jnp.float32)
        keys = keys.reshape(-1, keys.shape[2]).astype(jnp.bfloat16)
        contexts.append(
            context_of(
                jnp.concatenate([q_ref[t, n] for t in range(STEPS)], axis=0),
                lambda q: lax.dot_general(q, keys, NT, preferred_element_type=jnp.float32),
                lambda p: jnp.dot(p, keys[:, :LAT], preferred_element_type=jnp.float32),
                fresh_ref[n],
                len_ref[n],
            )
        )
    rows = resident + fresh_rows
    context = jnp.concatenate(contexts, axis=0)
    size = context.shape[0]
    heads = queries // STEPS
    to = lax.broadcasted_iota(jnp.int32, (size, size), 0)
    source = to % rows * queries + to // rows % STEPS * heads + to // (rows * STEPS)
    turn = (source == lax.broadcasted_iota(jnp.int32, (size, size), 1)).astype(jnp.float32)
    turned = jnp.dot(turn.astype(jnp.bfloat16), context, preferred_element_type=jnp.float32)
    out_ref[...] = turned.reshape(out_ref.shape).astype(jnp.bfloat16)


def attend_new(lengths, queries, taken, fresh, done, columns, ready):
    _, rows, _, width = taken.shape
    steps, whole, heads, _ = queries.shape
    out = (columns, heads // columns, steps * whole, LAT)
    last = whole // rows - 1
    return pl.pallas_call(
        functools.partial(attend_new_body, len(done)),
        grid=(1,),
        in_specs=[
            pl.BlockSpec(memory_space=pltpu.SMEM),
            pl.BlockSpec((steps, rows, heads, width), lambda i: (0, last, 0, 0)),
            pl.BlockSpec(taken.shape, lambda i: (0, 0, 0, 0)),
            pl.BlockSpec((rows, *fresh.shape[1:]), lambda i: (last, 0, 0)),
            *[pl.BlockSpec(d.shape, lambda i: (0, 0, 0)) for d in done],
        ]
        + [pl.BlockSpec(memory_space=pltpu.HBM)] * len(ready),
        out_specs=pl.BlockSpec(out, lambda i: (0, 0, 0, 0)),
        out_shape=jax.ShapeDtypeStruct(out, jnp.bfloat16),
        compiler_params=pltpu.CompilerParams(vmem_limit_bytes=24 * 1024 * 1024),
        cost_estimate=pl.CostEstimate(
            flops=4 * taken.size * steps * heads, bytes_accessed=20000000, transcendentals=0
        ),
        name="attend_new",
    )(lengths, queries, taken, fresh, *done, *ready)


def picked(one_hot, x, dims=(((1,), (0,)), ((), ()))):
    one_hot = one_hot.astype(jnp.float32).astype(jnp.bfloat16)
    total = None
    for _ in range(3):
        part = x.astype(jnp.bfloat16)
        x = x - part.astype(jnp.float32)
        term = lax.dot_general(one_hot, part, dims, preferred_element_type=jnp.float32)
        total = term if total is None else total + term
    return total


def routing_body(sizes, place_ref, ids_ref, weights_ref, *refs):
    long, short, rows_dev = sizes
    select_ref, own_ref, spread_ref, present_ref, weight_ref = refs[-5:]
    steps, _, rows = ids_ref.shape
    columns = long * short
    own_rows, slots = steps * rows_dev, steps * CAP
    at_y, at_x = place_ref[2], place_ref[3]

    def iota(shape, axis):
        return lax.broadcasted_iota(jnp.int32, shape, axis)

    for t in range(steps):
        ids, weights = ids_ref[t], weights_ref[t]
        for e in range(columns):
            at = slice(e * steps + t, e * steps + t + 1)
            matched = ids == e
            present_ref[at] = jnp.max(matched.astype(jnp.float32), axis=0, keepdims=True)
            weight_ref[at] = jnp.sum(jnp.where(matched, weights, 0.0), axis=0, keepdims=True)
    present = present_ref[...]
    before = iota((rows, rows), 0) < iota((rows, rows), 1)
    place = jnp.dot(
        present.astype(jnp.bfloat16),
        before.astype(jnp.float32).astype(jnp.bfloat16),
        preferred_element_type=jnp.float32,
    )
    count = columns * slots
    widen = iota((count, columns * steps), 0) // CAP == iota((count, columns * steps), 1)
    slot = (iota((count, rows), 0) % CAP).astype(jnp.float32)
    chosen = (picked(widen, place) == slot) & (picked(widen, present) > 0.5)
    weighted = jnp.where(chosen, picked(widen, weight_ref[...]), 0.0)
    total = columns * own_rows
    to = iota((rows, total), 1)
    spot = to // own_rows * rows_dev + to % rows_dev == iota((rows, total), 0)
    same = (
        iota((count, total), 0) // CAP % steps == iota((count, total), 1) // rows_dev % steps
    )
    spot = spot.astype(jnp.float32).astype(jnp.bfloat16)
    chooser = jnp.dot(
        chosen.astype(jnp.float32).astype(jnp.bfloat16), spot, preferred_element_type=jnp.float32
    )
    chooser = jnp.where(same, chooser, 0.0).astype(jnp.bfloat16)
    select_ref[:count] = chooser
    to = iota((total, total), 0)
    from_x = (at_x + to // (long * own_rows)) % short
    from_y = (at_y + to // own_rows % long) % long
    source = (from_y * short + from_x) * own_rows + to % own_rows
    turned = source == iota((total, total), 1)
    select_ref[count:] = turned.astype(jnp.float32).astype(jnp.bfloat16)
    head = at_y * short + at_x
    mine = iota((total, own_rows), 0) == head * own_rows + iota((total, own_rows), 1)
    own_ref[...] = jnp.dot(
        chooser, mine.astype(jnp.float32).astype(jnp.bfloat16), preferred_element_type=jnp.float32
    ).astype(jnp.bfloat16)
    to = iota((short * slots, count), 0)
    expert = at_y * short + (at_x + short - to // slots) % short
    near = picked(expert * slots + to % slots == iota((short * slots, count), 1), weighted)
    to = iota((long * own_rows, rows), 0)
    row = ((at_y + to // own_rows) % long * short + at_x) * rows_dev + to % rows_dev
    near = picked(row == iota((long * own_rows, rows), 1), near, NT)
    shape = (long * own_rows, short * slots)
    same = iota(shape, 0) // rows_dev % steps == iota(shape, 1) // CAP % steps
    spread_ref[...] = jnp.where(same, near, 0.0)


def routing(place, ids, weights, long, short, rows_dev, ready):
    steps, _, rows = ids.shape
    count, total = long * short * steps * CAP, rows * steps
    vmem = pl.BlockSpec(memory_space=pltpu.VMEM)
    return pl.pallas_call(
        functools.partial(routing_body, (long, short, rows_dev)),
        in_specs=[
            pl.BlockSpec(memory_space=pltpu.SMEM),
            vmem,
            vmem,
            *[pl.BlockSpec(memory_space=pltpu.HBM)] * len(ready),
        ],
        out_specs=[vmem] * 3,
        out_shape=[
            jax.ShapeDtypeStruct((count + total, total), jnp.bfloat16),
            jax.ShapeDtypeStruct((count, steps * rows_dev), jnp.bfloat16),
            jax.ShapeDtypeStruct((long * steps * rows_dev, short * steps * CAP), jnp.float32),
        ],
        scratch_shapes=[pltpu.VMEM((long * short * steps, rows), jnp.float32)] * 2,
        compiler_params=pltpu.CompilerParams(vmem_limit_bytes=24 * 1024 * 1024),
        cost_estimate=pl.CostEstimate(flops=0, bytes_accessed=100000, transcendentals=0),
        name="routing",
    )(place, ids, weights, *ready)


def after_body(up_ref, down_ref, ready_ref, out_up_ref, out_down_ref, pair_ref):
    del ready_ref
    for k, (ref, out_ref) in enumerate([(up_ref, out_up_ref), (down_ref, out_down_ref)]):
        block = ref[...]
        out_ref[...] = block
        pair_ref[k] = block


def after(up, down, ready, space):
    vmem = pl.BlockSpec(memory_space=pltpu.VMEM)
    one = jax.ShapeDtypeStruct(up.shape, up.dtype)
    return pl.pallas_call(
        after_body,
        in_specs=[vmem, vmem, pl.BlockSpec(memory_space=space)],
        out_specs=[vmem] * 3,
        out_shape=[one, one, jax.ShapeDtypeStruct((2, *up.shape), up.dtype)],
        compiler_params=pltpu.CompilerParams(vmem_limit_bytes=8 * 1024 * 1024),
        cost_estimate=pl.CostEstimate(flops=0, bytes_accessed=100000, transcendentals=0),
        name="after",
    )(up, down, ready)


def halves_body(up_ref, down_ref, ready_ref, first_ref, second_ref):
    del ready_ref
    half = first_ref.shape[0]
    first_ref[...] = up_ref[:half]
    second_ref[...] = down_ref[half:]


def halves(up, down, ready):
    vmem = pl.BlockSpec(memory_space=pltpu.VMEM)
    half = jax.ShapeDtypeStruct((up.shape[0] // 2, up.shape[1]), up.dtype)
    return pl.pallas_call(
        halves_body,
        in_specs=[vmem] * 3,
        out_specs=[vmem] * 2,
        out_shape=[half, half],
        compiler_params=pltpu.CompilerParams(vmem_limit_bytes=8 * 1024 * 1024),
        cost_estimate=pl.CostEstimate(flops=0, bytes_accessed=100000, transcendentals=0),
        name="halves",
    )(up, down, ready)


def project_body(layout, place_ref, by_ref, uv_ref, select_ref, own_ref, hidden_ref, *refs):
    total = 1 + max(i for pair in layout for parts in pair for i, _ in parts)
    blocks, outs = refs[:total], refs[total:-5]
    held, slots_ref, rows_ref, sems, out_sems = refs[-5:]
    chips = len(layout)
    copies, start = [], 0
    for pair in layout:
        for i, j in pair[0] + pair[1]:
            r = blocks[i] if j is None else blocks[i].at[j]
            size = r.shape[0]
            copies.append(
                pltpu.make_async_copy(r, held.at[pl.ds(start, size)], sems.at[len(copies)])
            )
            copies[-1].start()
            start += size
    values = []
    for k in range(uv_ref.shape[0]):
        context = by_ref[:, k].astype(jnp.float32).reshape(-1, by_ref.shape[3])
        values.append(
            jnp.dot(context.astype(jnp.bfloat16), uv_ref[k], preferred_element_type=jnp.float32)
        )
    values = jnp.concatenate(values, axis=1).astype(jnp.bfloat16)
    x = jnp.dot(select_ref[...], values, preferred_element_type=jnp.float32).astype(jnp.bfloat16)
    half = slots_ref.shape[0]
    each = rows_ref.shape[1]
    first = place_ref[1] == 0
    at, start = 0, 0
    width = held.shape[0] // chips
    core_width = width // 2
    leaving = []
    for k, (ours, theirs) in enumerate(layout):
        for _ in ours + theirs:
            copies[at].wait()
            at += 1
        pair = [
            lax.dot_general(
                x,
                held[start + c * core_width : start + (c + 1) * core_width],
                NT,
                preferred_element_type=jnp.float32,
            )
            for c in range(2)
        ]
        start += width
        whole = jnp.concatenate(
            [jnp.where(first, pair[0], pair[1]), jnp.where(first, pair[1], pair[0])], axis=1
        )
        chip = lax.rem(place_ref[0] + (chips - k), chips)
        columns = pl.ds(pl.multiple_of(chip * width, 128), width)
        carried = jnp.dot(own_ref[...], hidden_ref[:, columns], preferred_element_type=jnp.float32)
        slots_ref[:, columns] = (whole[:half] + carried).astype(jnp.bfloat16)
        for j in range(rows_ref.shape[0]):
            row = half + j * each
            rows_ref[j, :, columns] = whole[row : row + each].astype(jnp.bfloat16)
        for j, out_ref in enumerate(outs):
            source = slots_ref if j == 0 else rows_ref.at[j - 1]
            leaving.append(
                pltpu.make_async_copy(
                    source.at[:, columns], out_ref.at[:, columns], out_sems.at[j, k]
                )
            )
            leaving[-1].start()
    for copy in leaving:
        copy.wait()


def project(place, by_head, w_uv, select, blocks, layout, chooser, hidden, outer, inner):
    rows, depth = select.shape[0], blocks[0].shape[1]
    half = rows // 2
    width = sum(part.size for part in blocks) // depth
    parts = sum(len(a) + len(b) for a, b in layout)
    each = half // inner
    vmem = pl.BlockSpec(memory_space=pltpu.VMEM)
    anywhere = pl.BlockSpec(memory_space=pltpu.HBM)
    return pl.pallas_call(
        functools.partial(project_body, layout),
        in_specs=[pl.BlockSpec(memory_space=pltpu.SMEM)] + [vmem] * 5 + [anywhere] * len(blocks),
        out_specs=[anywhere] * (1 + inner),
        out_shape=[jax.ShapeDtypeStruct((half, width), jnp.bfloat16)]
        + [jax.ShapeDtypeStruct((each, width), jnp.bfloat16)] * inner,
        scratch_shapes=[
            pltpu.VMEM((width, depth), jnp.bfloat16),
            pltpu.VMEM((half, width), jnp.bfloat16),
            pltpu.VMEM((inner, each, width), jnp.bfloat16),
            pltpu.SemaphoreType.DMA((parts,)),
            pltpu.SemaphoreType.DMA((1 + inner, len(layout))),
        ],
        compiler_params=pltpu.CompilerParams(vmem_limit_bytes=63200000),
        cost_estimate=pl.CostEstimate(
            flops=2 * rows * depth * width,
            bytes_accessed=2 * depth * width + 2 * rows * width,
            transcendentals=0,
        ),
        name="project",
    )(place, by_head, w_uv, select, chooser, hidden, *blocks)


def norm_body(parts_ref, gain_ref, *refs):
    total, out_ref = refs[-1], refs[(len(refs) - 2) // 2]
    parts, _, width = parts_ref.shape
    tile = width // 8
    squares = 0.0
    for k in range(8):
        at = slice(k * tile, (k + 1) * tile)
        here = parts_ref[0, :, at].astype(jnp.float32)
        for j in range(1, parts):
            here += parts_ref[j, :, at].astype(jnp.float32)
        total[:, at] = here
        squares += jnp.sum(here * here, axis=1, keepdims=True)
    scale = lax.rsqrt(squares * (1.0 / width) + 1e-06)
    for k in range(8):
        at = slice(k * tile, (k + 1) * tile)
        out_ref[:, at] = (total[:, at] * scale * gain_ref[:, at]).astype(jnp.bfloat16)


def norm(parts, gain, held):
    _, rows, width = parts.shape
    vmem = pl.BlockSpec(memory_space=pltpu.VMEM)
    anywhere = pl.BlockSpec(memory_space=pltpu.HBM)
    return pl.pallas_call(
        norm_body,
        in_specs=[vmem, vmem] + [anywhere] * len(held),
        out_specs=[vmem] + [anywhere] * len(held),
        out_shape=[jax.ShapeDtypeStruct((rows, width), jnp.bfloat16)]
        + [jax.ShapeDtypeStruct(h.shape, h.dtype) for h in held],
        scratch_shapes=[pltpu.VMEM((rows, width), jnp.float32)],
        input_output_aliases={2 + k: 1 + k for k in range(len(held))},
        compiler_params=pltpu.CompilerParams(vmem_limit_bytes=16 * 1024 * 1024),
        cost_estimate=pl.CostEstimate(
            flops=2 * parts.size, bytes_accessed=2 * parts.size, transcendentals=0
        ),
        name="norm",
    )(parts, gain, *held)


def gate_up_body(core_ref, x_ref, own_ref, other_ref, *refs):
    active_ref, gate, up = refs[-3:]
    step = pl.program_id(0)

    @pl.when(step == 0)
    def _():
        gate[...] = jnp.zeros_like(gate)
        up[...] = jnp.zeros_like(up)

    x = x_ref[...]
    for part, total in ((0, gate), (1, up)):
        both = jnp.concatenate([own_ref[part], other_ref[part]], axis=1)
        total[...] += jnp.dot(x, both, preferred_element_type=jnp.float32)

    @pl.when(step == pl.num_programs(0) - 1)
    def _():
        g = gate[...]
        active = (g * jax.nn.sigmoid(g) * up[...]).astype(jnp.bfloat16)
        units = active.shape[1] // 2
        first, second = active[:, :units], active[:, units:]

        @pl.when(core_ref[0] == 0)
        def _():
            for k in range(active_ref.shape[0]):
                active_ref[k, :, :units] = first
                active_ref[k, :, units:] = second

        @pl.when(core_ref[0] != 0)
        def _():
            for k in range(active_ref.shape[0]):
                active_ref[k, :, :units] = second
                active_ref[k, :, units:] = first


def gate_up(core, x, own, other, copies, ready):
    rows, depth = x.shape
    units = own.shape[2]
    tile = depth // 2
    return pl.pallas_call(
        gate_up_body,
        grid=(depth // tile,),
        in_specs=[
            pl.BlockSpec(memory_space=pltpu.SMEM),
            pl.BlockSpec((rows, tile), lambda i: (0, i)),
            pl.BlockSpec((2, tile, units), lambda i: (0, i, 0)),
            pl.BlockSpec((2, tile, units), lambda i: (0, i, 0)),
            *[pl.BlockSpec(memory_space=pltpu.HBM)] * len(ready),
        ],
        out_specs=pl.BlockSpec((copies, rows, 2 * units), lambda i: (0, 0, 0)),
        out_shape=jax.ShapeDtypeStruct((copies, rows, 2 * units), jnp.bfloat16),
        scratch_shapes=[pltpu.VMEM((rows, 2 * units), jnp.float32)] * 2,
        compiler_params=pltpu.CompilerParams(vmem_limit_bytes=24 * 1024 * 1024),
        cost_estimate=pl.CostEstimate(
            flops=8 * rows * depth * units,
            bytes_accessed=8 * depth * units + 2 * rows * depth,
            transcendentals=2 * rows * units,
        ),
        name="gate_up",
    )(core, x, own, other, *ready)


def down_body(core_ref, x_ref, own_ref, other_ref, out_ref, held, sems):
    copies = [
        pltpu.make_async_copy(r, held.at[k], sems.at[k]) for k, r in enumerate((own_ref, other_ref))
    ]
    for copy in copies:
        copy.start()
    x = jnp.concatenate([x_ref[k] for k in range(x_ref.shape[0])], axis=1)
    half = own_ref.shape[0]
    parts, each = out_ref.shape[0], out_ref.shape[1]
    copies[0].wait()
    mine = lax.dot_general(x, held[0], NT, preferred_element_type=jnp.float32)
    copies[1].wait()
    others = lax.dot_general(x, held[1], NT, preferred_element_type=jnp.float32)

    def write(first, second):
        both = jnp.concatenate([first, second], axis=1).reshape(parts, each, 2 * half)
        out_ref[...] = both.astype(jnp.bfloat16)

    @pl.when(core_ref[0] == 0)
    def _():
        write(mine, others)

    @pl.when(core_ref[0] != 0)
    def _():
        write(others, mine)


def down_project(core, x, own, other):
    parts, rows, _ = x.shape
    columns = 2 * own.shape[0]
    vmem = pl.BlockSpec(memory_space=pltpu.VMEM)
    return pl.pallas_call(
        down_body,
        in_specs=[
            pl.BlockSpec(memory_space=pltpu.SMEM),
            vmem,
            *[pl.BlockSpec(memory_space=pltpu.HBM)] * 2,
        ],
        out_specs=vmem,
        out_shape=jax.ShapeDtypeStruct((parts, rows // parts, columns), jnp.bfloat16),
        scratch_shapes=[
            pltpu.VMEM((2, *own.shape), own.dtype),
            pltpu.SemaphoreType.DMA((2,)),
        ],
        compiler_params=pltpu.CompilerParams(vmem_limit_bytes=24 * 1024 * 1024),
        cost_estimate=pl.CostEstimate(
            flops=2 * rows * own.shape[1] * columns,
            bytes_accessed=2 * own.shape[1] * columns,
            transcendentals=0,
        ),
        name="down_project",
    )(core, x, own, other)


def combine_body(count, spread_ref, hidden_ref, *refs):
    blocks, sums, (here_ref, *away) = refs[:count], refs[count : 2 * count], refs[2 * count :]
    weight = spread_ref[...]
    high = weight.astype(jnp.bfloat16)
    low = (weight - high.astype(jnp.float32)).astype(jnp.bfloat16)
    parts, _, width = blocks[0].shape
    each = here_ref.shape[0]
    for k in range(parts):
        slots = jnp.concatenate([b[k].astype(jnp.float32) for b in blocks], axis=0)
        slots = slots.astype(jnp.bfloat16)
        mixed = jnp.dot(high, slots, preferred_element_type=jnp.float32) + jnp.dot(
            low, slots, preferred_element_type=jnp.float32
        )
        at = slice(k * width, (k + 1) * width)
        for r in sums:
            mixed += r[:, at].astype(jnp.float32)
        for y in range(1 + len(away)):
            row = mixed[y * each : (y + 1) * each]
            if y == 0:
                here_ref[:, at] = row + hidden_ref[:, at].astype(jnp.float32)
            else:
                away[y - 1][:, at] = row.astype(jnp.bfloat16)


def combine(spread, hidden, blocks, sums):
    each, width = hidden.shape
    outer = spread.shape[0] // each
    vmem = pl.BlockSpec(memory_space=pltpu.VMEM)
    away = jax.ShapeDtypeStruct((each, width), jnp.bfloat16)
    return pl.pallas_call(
        functools.partial(combine_body, len(blocks)),
        in_specs=[vmem] * (2 + len(blocks) + len(sums)),
        out_specs=[vmem] * outer,
        out_shape=[jax.ShapeDtypeStruct((each, width), jnp.float32)] + [away] * (outer - 1),
        compiler_params=pltpu.CompilerParams(vmem_limit_bytes=16 * 1024 * 1024),
        cost_estimate=pl.CostEstimate(
            flops=4 * spread.shape[0] * spread.shape[1] * width,
            bytes_accessed=10 * spread.shape[0] * width,
            transcendentals=0,
        ),
        name="combine",
    )(spread, hidden, *blocks, *sums)


def finish_body(here_ref, *refs):
    *parts, out_ref = refs
    total = here_ref[...]
    for r in parts:
        total += r[...].astype(jnp.float32)
    steps, rows, _ = out_ref.shape
    for t in range(steps):
        out_ref[t] = total[t * rows : (t + 1) * rows].astype(jnp.bfloat16)


def finish(here, parts, steps):
    rows, width = here.shape
    vmem = pl.BlockSpec(memory_space=pltpu.VMEM)
    return pl.pallas_call(
        finish_body,
        in_specs=[vmem] * (1 + len(parts)),
        out_specs=vmem,
        out_shape=jax.ShapeDtypeStruct((steps, rows // steps, width), jnp.bfloat16),
        compiler_params=pltpu.CompilerParams(vmem_limit_bytes=8 * 1024 * 1024),
        name="finish",
    )(here, *parts)


def shifted(x, axis, by):
    size = lax.axis_size(axis)
    return lax.ppermute(x, axis, [(i, (i + by) % size) for i in range(size)])


def swap_cores(x):
    return lax.ppermute(x, "core", [(0, 1), (1, 0)])


def per_device(
    hidden_in,
    queries,
    fresh,
    res_cache,
    res_len,
    pre_cache,
    pre_len,
    arrival,
    w_uv,
    w_o,
    norm_gain,
    expert_ids,
    route_weight,
    w_gu,
    w_down,
):
    group, head = ("z", "core"), ("y", "x")
    chips, cores, long, short = (lax.axis_size(a) for a in ("z", "core", "y", "x"))
    groups, columns = chips * cores, long * short
    core, at_y, at_x = (lax.axis_index(a) for a in ("core", "y", "x"))
    group_index = lax.axis_index(group)
    steps, rows_dev, width = hidden_in.shape
    resident = res_cache.shape[0]
    newcomers = rows_dev - resident
    requests = arrival.shape[1]
    own_rows = steps * rows_dev
    slots_dev = steps * CAP

    place = jnp.stack([lax.axis_index("z"), core, at_y, at_x]).astype(jnp.int32)
    gu_other = swap_cores(w_gu[0])
    down = w_down[0].T
    down_other = swap_cores(down)

    places = jnp.arange(requests, dtype=jnp.int32)
    arrival_row = arrival[0]
    claimed = arrival_row[None, :] == places[:, None]
    order = jnp.sum(jnp.where(claimed, places[None, :], 0), axis=1)
    len_sorted = jnp.sum(jnp.where(claimed, pre_len[0][None, :], 0), axis=1)
    new_len = lax.dynamic_slice(len_sorted, (group_index * newcomers,), (newcomers,))
    sorted_cache = jnp.take(pre_cache[0], order, axis=0, mode="clip")
    taken = lax.all_to_all(
        sorted_cache.reshape(groups, newcomers, *sorted_cache.shape[1:]),
        group,
        split_axis=0,
        concat_axis=0,
        tiled=False,
    )
    recent = jnp.swapaxes(jnp.pad(fresh, ((0, 8 - steps), (0, 0), (0, 0))), 0, 1)
    by_width = jnp.swapaxes(res_cache, 1, 2)
    done = [attend_resident(k, res_len, queries, by_width, recent) for k in range(resident)]
    hidden_own = hidden_in.reshape(own_rows, width)
    block = w_o.T
    up, down_block, near = after(shifted(block, "z", 1), shifted(block, "z", -1), done[0], pltpu.VMEM)
    context = attend_new(new_len, queries, taken, recent, done, columns, [gu_other, down_other])
    select, own_chooser, spread = routing(
        place,
        jnp.swapaxes(expert_ids, 1, 2),
        jnp.swapaxes(route_weight, 1, 2),
        long,
        short,
        rows_dev,
        [context, hidden_own],
    )
    up, down_block, mid = after(
        shifted(up, "z", 1), shifted(down_block, "z", -1), context, pltpu.HBM
    )
    far = [shifted(up, "z", 1), shifted(down_block, "z", -1)]
    first, second = halves(*far, select)
    last = [shifted(first, "z", 1), shifted(second, "z", -1)]
    blocks = [block, near, mid, *far, *last]
    places = [[(0, None)], [(1, 0)], [(2, 0)], [(3, None)], [(5, None), (6, None)]]
    places += [[(4, None)], [(2, 1)], [(1, 1)]]
    assert len(places) == chips
    count = len(blocks)
    layout = [(parts, [(i + count, j) for i, j in parts]) for parts in places]
    blocks = blocks + [swap_cores(part) for part in blocks]
    by_head = lax.all_to_all(context, head, split_axis=0, concat_axis=0, tiled=False)
    part_slots, row_here, *row_away = project(
        place, by_head, w_uv, select, blocks, layout, own_chooser, hidden_own, long, short
    )
    slot_parts = lax.all_to_all(
        part_slots.reshape(columns, slots_dev, width), head, 0, 0, tiled=False
    )
    normed, *row_away = norm(slot_parts, norm_gain[None], row_away)
    row_parts = [row_here] + [shifted(r, "x", k + 1) for k, r in enumerate(row_away)]

    core_now = jnp.reshape(core, (1,)).astype(jnp.int32)
    portion = lax.all_gather(normed, "z", axis=0, tiled=True)
    active = gate_up(core_now, portion, w_gu[0], gu_other, chips, row_parts[1:])
    everywhere = lax.all_to_all(active, "z", 0, 0, tiled=False)
    outcome = down_project(core_now, everywhere, down, down_other)
    slot_values = lax.all_to_all(outcome, "z", 0, 0, tiled=False)
    beside = [slot_values] + [shifted(slot_values, "x", k) for k in range(1, short)]
    out, *mixed = combine(spread, hidden_own, beside, row_parts)
    return finish(out, [shifted(part, "y", k + 1) for k, part in enumerate(mixed)], steps)


def solution(mesh):
    wide = Mesh(mesh.devices.reshape(8, 2, 4, 4), ("z", "core", "y", "x"))
    group, head = ("z", "core"), ("y", "x")
    both = group + head
    placed = (
        P(None, both, None),
        P(None, both, None, None),
        P(None, both, None),
        P(both, None, None),
        P(both),
        P(head, None, group, None),
        P(head, None),
        P(head, None),
        P(head, None, None),
        P(head, group),
        P(),
        P(None, group, None),
        P(None, group, None),
        P(head, None, None, group),
        P(head, None, group),
    )
    return jax.shard_map(
        per_device,
        mesh=wide,
        in_specs=placed,
        out_specs=P(None, both, None),
        check_vma=False,
    )
```
